256 devices in a mesh: row: 16 (over z, core), col: 16 (over y, x).
Axes of the slice: x: 4, y: 4, z: 8, core: 2. Of those that a mesh axis runs over, the one named last changes fastest.
Arguments:
- a_blocks: bfloat16 [256, 32, 128, 128], P('row', 'col'), may hold values from -0.5 to 0.5
- a_cols: int32 [256, 32], P('row', 'col'), may hold values from 0 to 255, as said below
- p_blocks: bfloat16 [256, 2, 128, 128], P(('row', 'col')), may hold values from -0.5 to 0.5
- p_aggs: int32 [256, 2], replicated, may hold values from 0 to 31, as said below
- agglo: int32 [32], replicated, may hold values from 0 to 31, as said below
Outputs:
- coarse_operator: float32 [32, 128, 6, 128], P('row', 'col')
The draws below stay inside these ranges and needn't reach their ends.
Inputs may be any that keep to these rules, and one draw needn't show every extreme that they name: `a_cols`: the entries of a block row are distinct, include the block row itself, and lie in block rows of the groups g - 1, g and g + 1 of the row's group g, groups of 16 block rows. `p_aggs`: each aggregate holds exactly 8 block rows, all of one group; the first entry of a block row is its own aggregate, the others are distinct further aggregates of the same group. `agglo`: within each group the 2 aggregates go to the group's 2 coarse block rows one to one.
All inputs are finite; a program needn't handle non-finite values.
Results may differ from the reference program's by a relative error of at most 0.0003.
Values may be sent and summed in bfloat16 or wider, within the bound.
No kernel may reach another device: no remote copies, remote signals or barrier semaphores. Data moves between devices by JAX's collectives and lax.ppermute only.
A program may use at most 64 MiB of HBM per device.

```python
import jax
import jax.numpy as jnp
from jax import lax

B = 128
AGG = 8
RB = 16
KP = 2
KA = 32
CR = 2
NB = 256
NCB = 32
N_ROW = 16


def draw_a_cols(key, part):
    row_ids = jnp.arange(NB)
    group_ids = row_ids // RB
    key_list = jax.random.split(jax.random.fold_in(key, 11), NB)
    orderings = jax.vmap(lambda single: jax.random.permutation(single, 3 * RB))(key_list)
    candidate = (group_ids[:, None] - 1) * RB + orderings
    usable = (candidate >= 0) & (candidate < NB) & (candidate != row_ids[:, None])
    ranking = jnp.where(usable, jnp.arange(3 * RB)[None, :], 10 * RB)
    chosen = jnp.argsort(ranking, axis=1)[:, :KA - 1]
    picked = jnp.take_along_axis(candidate, chosen, axis=1)
    columns = jnp.concatenate([row_ids[:, None], picked], axis=1)
    shuffle_keys = jax.random.split(jax.random.fold_in(key, 12), NB)
    shuffle = jax.vmap(lambda single: jax.random.permutation(single, KA))(shuffle_keys)
    return jnp.take_along_axis(columns, shuffle, axis=1).astype(jnp.int32)


def draw_p_aggs(key, part):
    group_total = NB // RB
    group_keys = jax.random.split(jax.random.fold_in(key, 21), group_total)
    orderings = jax.vmap(lambda single: jax.random.permutation(single, RB))(group_keys)
    aggregate = (orderings // AGG).reshape(NB)
    group_ids = jnp.arange(NB) // RB
    row_keys = jax.random.split(jax.random.fold_in(key, 22), NB)
    offsets = jax.vmap(lambda single: jax.random.permutation(single, CR - 1))(row_keys)[:, :KP - 1] + 1
    others = group_ids[:, None] * CR + (aggregate[:, None] + offsets) % CR
    own_ids = group_ids * CR + aggregate
    return jnp.concatenate([own_ids[:, None], others], axis=1).astype(jnp.int32)


def draw_agglo(key, part):
    group_total = NCB // CR
    group_keys = jax.random.split(jax.random.fold_in(key, 31), group_total)
    orderings = jax.vmap(lambda single: jax.random.permutation(single, CR))(group_keys)
    bases = jnp.arange(group_total)[:, None] * CR
    return (orderings + bases).reshape(NCB).astype(jnp.int32)


def level_of(stream_key, dims, cuts, smallest, largest):
    level = 1.0
    for dim, blocks in cuts:
        draws = jax.random.uniform(jax.random.fold_in(jax.random.fold_in(stream_key, 6), dim), (blocks,), jnp.float32, smallest / len(cuts), largest / len(cuts))
        level = level * jnp.repeat(jnp.exp(draws), dims[dim] // blocks).reshape((-1,) + (1,) * (len(dims) - 1 - dim))
    return level


def gaussian(stream_key, extent, width, limit, pieces=(), held_as=jnp.bfloat16):
    drawn = jax.random.normal(stream_key, extent, jnp.float32) * width
    if len(pieces) > 0:
        drawn = level_of(stream_key, extent, pieces, -0.22, 0.18) * drawn
    return jnp.clip(drawn, min=-limit, max=limit).astype(held_as)


def setup_inputs(seed: int = 0) -> dict:
    seeds = jax.random.split(jax.random.key(seed), 6)
    a_blocks = gaussian(seeds[0], (NB, KA, B, B), B ** -0.5, 0.5, ((0, 16), (1, 16)))
    a_cols = draw_a_cols(jax.random.fold_in(seeds[5], 71), 0)
    p_blocks = gaussian(seeds[2], (NB, KP, B, B), B ** -0.5, 0.5, ((0, 256),))
    p_aggs = draw_p_aggs(jax.random.fold_in(seeds[5], 71), 0)
    agglo = draw_agglo(jax.random.fold_in(seeds[5], 71), 0)
    return dict(a_blocks=a_blocks, a_cols=a_cols, p_blocks=p_blocks, p_aggs=p_aggs, agglo=agglo)


def reference(a_blocks, a_cols, p_blocks, p_aggs, agglo):
    highest = lax.Precision.HIGHEST
    coarse_ids = agglo[p_aggs]

    def group_block(group_id):
        first_row = (group_id * RB).astype(jnp.int32)
        rows_a = lax.dynamic_slice_in_dim(a_blocks, first_row, RB, 0).astype(jnp.float32)
        columns = lax.dynamic_slice_in_dim(a_cols, first_row, RB, 0)
        fetched = p_blocks[columns].astype(jnp.float32)
        products = jnp.einsum("isab,isqbc->isqac", rows_a, fetched, precision=highest)
        column_band = coarse_ids[columns] - (group_id - 1) * CR
        column_hot = (column_band[..., None] == jnp.arange(3 * CR)).astype(jnp.float32)
        applied = jnp.einsum("isqj,isqac->iajc", column_hot, products, precision=highest)
        own_blocks = lax.dynamic_slice_in_dim(p_blocks, first_row, RB, 0).astype(jnp.float32)
        row_band = lax.dynamic_slice_in_dim(coarse_ids, first_row, RB, 0) - group_id * CR
        row_hot = (row_band[..., None] == jnp.arange(CR)).astype(jnp.float32)
        selected = jnp.einsum("iqk,iqab->ikab", row_hot, own_blocks, precision=highest)
        return jnp.einsum("ikab,iajc->kbjc", selected, applied, precision=highest)

    blocks_all = lax.map(group_block, jnp.arange(N_ROW, dtype=jnp.int32))
    return blocks_all.reshape(NCB, B, 3 * CR, B)
```

```python
import jax
import jax.numpy as jnp
from jax import lax
from jax.experimental import pallas as pl
from jax.experimental.pallas import tpu as pltpu
from jax.sharding import PartitionSpec as P

ROWS = 16
SIDE = 4
B = 128
BOTH = ("row", "col")


def moved(even, odd):
    pairs = []
    for r in range(ROWS):
        dy, dx = (even, odd)[r % 2]
        for y in range(SIDE):
            for x in range(SIDE):
                target = ((y + dy) % SIDE) * SIDE + (x + dx) % SIDE
                pairs.append((r * ROWS + y * SIDE + x, r * ROWS + target))
    return pairs


def first(step):
    return moved((0, step), (step, 0))


def second(step):
    return moved((step, 0), (0, step))


def row_pairs(start):
    pairs = []
    for r in range(start, ROWS - 1, 2):
        pairs += [(r, r + 1), (r + 1, r)]
    return pairs


def place():
    row = lax.axis_index("row")
    col = lax.axis_index("col")
    return row, row % 2, col // SIDE, col % SIDE


def slot_of(y, x, y2, x2, core):
    dy, dx = (y - y2) & 3, (x - x2) & 3
    return jnp.where(core == 0, dy * SIDE + dx, dx * SIDE + dy)


def coarse_kernel(cols, aggs, agglo, a, w, o0, o1, o2, o3, split, acc):
    row, core, y, x = place()

    def parity(j):
        return agglo[aggs[j, 0]] & 1

    acc[...] = jnp.zeros_like(acc)

    def lift(i, carry):
        swap = parity(row * ROWS + i)
        spot = slot_of(y, x, i // SIDE, i % SIDE, core) * 4
        left = jnp.concatenate([w[spot + swap], w[spot + 1 - swap]], axis=1)
        right = jnp.concatenate([a[i, 0], a[i, 1]], axis=1)
        lifted = lax.dot_general(
            left, right, (((0,), (0,)), ((), ())), preferred_element_type=jnp.float32
        )
        high = lifted.astype(jnp.bfloat16)
        low = (lifted - high.astype(jnp.float32)).astype(jnp.bfloat16)
        for s in range(2):
            split[i * 2 + s, :, :B] = high[:, s * B : (s + 1) * B]
            split[i * 2 + s, :, B:] = low[:, s * B : (s + 1) * B]
        return carry

    lax.fori_loop(0, ROWS, lift, 0, unroll=4)

    def add(i, carry):
        for s in range(2):
            j = cols[i, s]
            swap = parity(j)
            band = j // ROWS - row + 1
            y2, x2 = (j % ROWS) // SIDE, j % SIDE
            mine = slot_of(y, x, y2, x2, core) * 4 + jnp.where(band == 1, 0, 2)
            theirs = slot_of(y, x, y2, x2, 1 - core) * 2
            use_pair = band == jnp.where(core == 0, 2, 0)
            spot = jnp.where(use_pair, 64 + theirs, mine)
            right = jnp.concatenate([w[spot + swap], w[spot + 1 - swap]], axis=1)
            right = jnp.concatenate([right, right], axis=0)
            acc[band] += jnp.dot(split[i * 2 + s], right, preferred_element_type=jnp.float32)
        return carry

    lax.fori_loop(0, ROWS, add, 0, unroll=4)

    for rel, out in enumerate((o0, o1, o2, o3)):
        for m in range(SIDE):
            d = jnp.where(
                core == 0,
                ((y + m) & 3) * SIDE + ((x + rel) & 3),
                ((y + rel) & 3) * SIDE + ((x + m) & 3),
            )
            for k in range(2):
                start = pl.multiple_of(k * B + d * 8, 8)
                for t in range(3):
                    out[m, k, :, t * 256 : (t + 1) * 256] = acc[t, pl.ds(start, 8), :]


def finish_kernel(kept, f, d, b, out):
    for k in range(2):
        total = kept[k] + f[k] + d[k] + b[k]
        for j in range(6):
            out[k, j] = total[:, j * B : (j + 1) * B]


def vmem():
    return pl.BlockSpec(memory_space=pltpu.VMEM)


def smem():
    return pl.BlockSpec(memory_space=pltpu.SMEM)


def local(a_blocks, a_cols, p_blocks, p_aggs, agglo):
    shard = p_blocks[0]
    beside = lax.ppermute(shard, "row", row_pairs(1))
    line = jnp.stack([shard, beside])
    line_f = lax.ppermute(line, BOTH, first(1))
    line_b = lax.ppermute(line, BOTH, first(-1))
    line_d = lax.ppermute(line, BOTH, first(2))
    line = jnp.stack([line, line_f, line_d, line_b])
    plane_f = lax.ppermute(line, BOTH, second(1))
    plane_b = lax.ppermute(line, BOTH, second(-1))
    plane_d = lax.ppermute(line, BOTH, second(2))
    plane = jnp.stack([line, plane_f, plane_d, plane_b])
    own = plane[:, :, 0].reshape(32, B, B)
    pair = lax.ppermute(own, "row", row_pairs(0))
    blocks = jnp.concatenate([plane.reshape(64, B, B), pair])

    piece = jax.ShapeDtypeStruct((SIDE, 2, 8, 768), jnp.float32)
    o0, o1, o2, o3 = pl.pallas_call(
        coarse_kernel,
        out_shape=[piece] * 4,
        in_specs=[smem(), smem(), smem(), vmem(), vmem()],
        out_specs=[vmem()] * 4,
        scratch_shapes=[
            pltpu.VMEM((32, 256, 256), jnp.bfloat16),
            pltpu.VMEM((3, 256, 256), jnp.float32),
        ],
        compiler_params=pltpu.CompilerParams(vmem_limit_bytes=24 * 2**20),
        name="coarse",
    )(a_cols, p_aggs, agglo, a_blocks, blocks)

    f = lax.ppermute(o1, BOTH, first(1))
    b = lax.ppermute(o3, BOTH, first(-1))
    d = lax.ppermute(o2, BOTH, first(2))
    line_sum = o0 + f + d + b
    f = lax.ppermute(line_sum[1], BOTH, second(1))
    b = lax.ppermute(line_sum[3], BOTH, second(-1))
    d = lax.ppermute(line_sum[2], BOTH, second(2))
    out = pl.pallas_call(
        finish_kernel,
        out_shape=jax.ShapeDtypeStruct((2, 6, 8, B), jnp.float32),
        in_specs=[vmem()] * 4,
        out_specs=vmem(),
        name="finish",
    )(line_sum[0], f, d, b)
    return out.transpose(0, 2, 1, 3)


def solution(mesh):
    placed = (
        P("row", "col", None, None),
        P("row", "col"),
        P(("row", "col"), None, None, None),
        P(),
        P(),
    )
    return jax.shard_map(
        local, mesh=mesh, in_specs=placed, out_specs=P("row", "col", None, None), check_vma=False
    )
```

```python
import jax
import jax.numpy as jnp
from jax import lax
from jax.experimental import pallas as pl
from jax.experimental.pallas import tpu as pltpu
from jax.sharding import PartitionSpec as P

ROWS = 16
SIDE = 4
B = 128
CHUNK = 4
BOTH = ("row", "col")


def moved(even, odd, rows=range(ROWS)):
    pairs = []
    for r in rows:
        dy, dx = (even, odd)[r % 2]
        for y in range(SIDE):
            for x in range(SIDE):
                target = ((y + dy) % SIDE) * SIDE + (x + dx) % SIDE
                pairs.append((r * ROWS + y * SIDE + x, r * ROWS + target))
    return pairs


def first(step, rows=range(ROWS)):
    return moved((0, step), (step, 0), rows)


def second(step):
    return moved((step, 0), (0, step))


def row_pairs(start):
    pairs = []
    for r in range(start, ROWS - 1, 2):
        pairs += [(r, r + 1), (r + 1, r)]
    return pairs


def place():
    row = lax.axis_index("row")
    col = lax.axis_index("col")
    return row, row % 2, col // SIDE, col % SIDE


def slot_of(y, x, j, core):
    dy, dx = (y - (j % ROWS) // SIDE) & 3, (x - j % SIDE) & 3
    return jnp.where(core == 0, dy * SIDE + dx, dx * SIDE + dy)


def parity(aggs, agglo, j):
    return agglo[aggs[j, 0]] & 1


def gather_products(band, core, y, x, row, cols, aggs, agglo, order, blocks, split):
    def scan(e, count):
        j = cols[e // 2, e % 2]

        @pl.when(j // ROWS - row + 1 == band)
        def _():
            order[0, count] = e
            spot = slot_of(y, x, j, core) * 2
            swap = parity(aggs, agglo, j)
            order[1, count] = spot + swap
            order[2, count] = spot + 1 - swap

        return count + (j // ROWS - row + 1 == band).astype(jnp.int32)

    count = lax.fori_loop(0, 2 * ROWS, scan, 0)
    for c in range(CHUNK - 1):
        order[0, count + c] = 2 * ROWS
        order[1, count + c] = 0
        order[2, count + c] = 0

    def chunk(c, total):
        left, right = [], []
        for u in range(CHUNK):
            p = c * CHUNK + u
            left.append(split[order[0, p]])
            one = jnp.concatenate([blocks[order[1, p]], blocks[order[2, p]]], axis=1)
            right += [one, one]
        return total + jnp.dot(
            jnp.concatenate(left, axis=1),
            jnp.concatenate(right, axis=0),
            preferred_element_type=jnp.float32,
        )

    return lax.fori_loop(
        0, (count + CHUNK - 1) // CHUNK, chunk, jnp.zeros((256, 256), jnp.float32)
    )


def own_kernel(cols, aggs, agglo, a, plane, split, acc, order):
    row, core, y, x = place()
    split[2 * ROWS] = jnp.zeros((256, 256), jnp.bfloat16)

    def lift(i, carry):
        swap = parity(aggs, agglo, row * ROWS + i)
        spot = slot_of(y, x, i, core) * 2
        left = jnp.concatenate([plane[spot + swap], plane[spot + 1 - swap]], axis=1)
        right = jnp.concatenate([a[i, 0], a[i, 1]], axis=1)
        lifted = lax.dot_general(
            left, right, (((0,), (0,)), ((), ())), preferred_element_type=jnp.float32
        )
        high = lifted.astype(jnp.bfloat16)
        low = (lifted - high.astype(jnp.float32)).astype(jnp.bfloat16)
        for s in range(2):
            split[i * 2 + s, :, :B] = high[:, s * B : (s + 1) * B]
            split[i * 2 + s, :, B:] = low[:, s * B : (s + 1) * B]
        return carry

    lax.fori_loop(0, ROWS, lift, 0, unroll=4)
    acc[...] = gather_products(1, core, y, x, row, cols, aggs, agglo, order, plane, split)


def pair_kernel(cols, aggs, agglo, split, pair, acc, order):
    row, core, y, x = place()
    band = 2 - 2 * core
    acc[...] = gather_products(band, 1 - core, y, x, row, cols, aggs, agglo, order, pair, split)


def beside_kernel(
    cols, aggs, agglo, split, n0, n1, n2, n3, acc_own, acc_pair, o0, o1, o2, o3, blocks, acc, order
):
    row, core, y, x = place()
    band = 2 * core
    for m, n in enumerate((n0, n1, n2, n3)):
        blocks[m * 8 : (m + 1) * 8] = n[...]
    acc[...] = gather_products(
        band, 1 - core, y, x, row, cols, aggs, agglo, order, blocks, split
    )
    for rel, out in enumerate((o0, o1, o2, o3)):
        for m in range(SIDE):
            d = jnp.where(
                core == 0,
                ((y + m) & 3) * SIDE + ((x + rel) & 3),
                ((y + rel) & 3) * SIDE + ((x + m) & 3),
            )
            for k in range(2):
                rows = pl.ds(pl.multiple_of(k * B + d * 8, 8), 8)
                out[m, k, :, 256:512] = acc_own[rows, :]
                beside, partner = acc[rows, :], acc_pair[rows, :]
                out[m, k, :, 0:256] = jnp.where(core == 0, beside, partner)
                out[m, k, :, 512:768] = jnp.where(core == 0, partner, beside)


def vmem():
    return pl.BlockSpec(memory_space=pltpu.VMEM)


def smem():
    return pl.BlockSpec(memory_space=pltpu.SMEM)


def local(a_blocks, a_cols, p_blocks, p_aggs, agglo):
    inner = range(1, ROWS - 1)
    shard = p_blocks[0]
    f = lax.ppermute(shard, BOTH, first(1))
    b = lax.ppermute(shard, BOTH, first(-1))
    d = lax.ppermute(shard, BOTH, first(2))
    line = jnp.concatenate([shard, f, d, b])
    plane_d = lax.ppermute(line, BOTH, second(2))
    beside_0 = lax.ppermute(line, "row", row_pairs(1))
    plane_f = lax.ppermute(line, BOTH, second(1))
    plane_b = lax.ppermute(line, BOTH, second(-1))
    plane_d, beside_0 = lax.optimization_barrier((plane_d, beside_0))
    beside_f = lax.ppermute(beside_0, BOTH, first(1, inner))
    beside_b = lax.ppermute(beside_0, BOTH, first(-1, inner))
    beside_d = lax.ppermute(plane_d, "row", row_pairs(1))
    plane_f, plane_b, beside_0 = lax.optimization_barrier((plane_f, plane_b, beside_0))
    plane = jnp.concatenate([line, plane_f, plane_d, plane_b])
    pair = lax.ppermute(plane, "row", row_pairs(0))

    scalars = (a_cols, p_aggs, agglo)
    order = pltpu.SMEM((3, 40), jnp.int32)
    square = jax.ShapeDtypeStruct((256, 256), jnp.float32)
    split, acc_own = pl.pallas_call(
        own_kernel,
        out_shape=[jax.ShapeDtypeStruct((33, 256, 256), jnp.bfloat16), square],
        in_specs=[smem(), smem(), smem(), vmem(), vmem()],
        out_specs=[vmem()] * 2,
        scratch_shapes=[order],
        compiler_params=pltpu.CompilerParams(vmem_limit_bytes=24 * 2**20),
        cost_estimate=pl.CostEstimate(flops=10**6, bytes_accessed=2**12, transcendentals=0),
        name="own",
    )(*scalars, a_blocks, plane)
    acc_pair = pl.pallas_call(
        pair_kernel,
        out_shape=square,
        in_specs=[smem(), smem(), smem(), vmem(), vmem()],
        out_specs=vmem(),
        scratch_shapes=[order],
        compiler_params=pltpu.CompilerParams(vmem_limit_bytes=24 * 2**20),
        cost_estimate=pl.CostEstimate(flops=10**6, bytes_accessed=2**12, transcendentals=0),
        name="pair",
    )(*scalars, split, pair)
    piece = jax.ShapeDtypeStruct((SIDE, 2, 8, 768), jnp.float32)
    o0, o1, o2, o3 = pl.pallas_call(
        beside_kernel,
        out_shape=[piece] * 4,
        in_specs=[smem(), smem(), smem()] + [vmem()] * 7,
        out_specs=[vmem()] * 4,
        scratch_shapes=[
            pltpu.VMEM((32, B, B), jnp.bfloat16),
            pltpu.VMEM((256, 256), jnp.float32),
            order,
        ],
        compiler_params=pltpu.CompilerParams(vmem_limit_bytes=24 * 2**20),
        cost_estimate=pl.CostEstimate(flops=10**6, bytes_accessed=2**12, transcendentals=0),
        name="beside",
    )(*scalars, split, beside_0, beside_f, beside_d, beside_b, acc_own, acc_pair)

    f = lax.ppermute(o1, BOTH, first(1))
    b = lax.ppermute(o3, BOTH, first(-1))
    d = lax.ppermute(o2, BOTH, first(2))
    kept, to_f, to_d, to_b = (o0[m] + f[m] + d[m] + b[m] for m in range(SIDE))
    f = lax.ppermute(to_f, BOTH, second(1))
    b = lax.ppermute(to_b, BOTH, second(-1))
    d = lax.ppermute(to_d, BOTH, second(2))
    return (kept + f + d + b).reshape(2, 8, 6, B)


def solution(mesh):
    placed = (
        P("row", "col", None, None),
        P("row", "col"),
        P(("row", "col"), None, None, None),
        P(),
        P(),
    )
    return jax.shard_map(
        local, mesh=mesh, in_specs=placed, out_specs=P("row", "col", None, None), check_vma=False
    )
```

```python
import jax
import jax.numpy as jnp
from jax import lax
from jax.experimental import pallas as pl
from jax.experimental.pallas import tpu as pltpu
from jax.sharding import PartitionSpec as P

ROWS = 16
SIDE = 4
B = 128
BOTH = ("row", "col")


def crossed(row):
    return (row + 1) // 2 % 2


def moved(along, step):
    pairs = []
    for r in range(ROWS):
        dy, dx = ((0, step), (step, 0))[crossed(r) ^ along]
        for y in range(SIDE):
            for x in range(SIDE):
                target = ((y + dy) % SIDE) * SIDE + (x + dx) % SIDE
                pairs.append((r * ROWS + y * SIDE + x, r * ROWS + target))
    return pairs


def first(step):
    return moved(0, step)


def second(step):
    return moved(1, step)


def row_pairs(start):
    pairs = []
    for r in range(start, ROWS - 1, 2):
        pairs += [(r, r + 1), (r + 1, r)]
    return pairs


def place():
    row = lax.axis_index("row")
    col = lax.axis_index("col")
    return row, crossed(row), col // SIDE, col % SIDE


def slot_of(y, x, j, cross):
    dy, dx = (y - (j % ROWS) // SIDE) & 3, (x - j % SIDE) & 3
    return jnp.where(cross == 0, dy * SIDE + dx, dx * SIDE + dy)


def fetch_kernel(a, shard, a_near, shard_near, sems):
    copies = [
        pltpu.make_async_copy(shard, shard_near, sems.at[0]),
        pltpu.make_async_copy(a, a_near, sems.at[1]),
    ]
    for copy in copies:
        copy.start()
    for copy in copies:
        copy.wait()


def lift_kernel(aggs, agglo, a, plane, split):
    row, cross, y, x = place()
    for i in range(ROWS):
        swap = agglo[aggs[0, row * ROWS + i]] & 1
        spot = slot_of(y, x, i, cross) * 2
        left = jnp.concatenate([plane[spot + swap], plane[spot + 1 - swap]], axis=1)
        right = jnp.concatenate([a[i, 0], a[i, 1]], axis=1)
        lifted = lax.dot_general(
            left, right, (((0,), (0,)), ((), ())), preferred_element_type=jnp.float32
        )
        high = lifted.astype(jnp.bfloat16)
        low = (lifted - high.astype(jnp.float32)).astype(jnp.bfloat16)
        for s in range(2):
            split[i * 2 + s, :, :B] = high[:, s * B : (s + 1) * B]
            split[i * 2 + s, :, B:] = low[:, s * B : (s + 1) * B]


def band_kernel(
    cols, aggs, agglo, split, plane, near, f, b, far, pair, o0, o1, o2, o3, blocks, acc
):
    row, cross, y, x = place()
    blocks[0:32] = plane[...]
    blocks[32:40] = near[...]
    blocks[40:48] = f[8:16]
    blocks[48:56] = far[...]
    blocks[56:64] = b[8:16]
    blocks[64:96] = pair[...]
    acc[...] = jnp.zeros_like(acc)
    pair_band = 2 - 2 * (row % 2)
    for i in range(ROWS):
        for s in range(2):
            j = cols[s, i]
            swap = agglo[aggs[0, j]] & 1
            band = j // ROWS - row + 1
            base = jnp.where(band == 1, 0, jnp.where(band == pair_band, 64, 32))
            spot = base + slot_of(y, x, j, jnp.where(band == pair_band, 1 - cross, cross)) * 2
            right = jnp.concatenate([blocks[spot + swap], blocks[spot + 1 - swap]], axis=1)
            right = jnp.concatenate([right, right], axis=0)
            acc[band] += jnp.dot(split[i * 2 + s], right, preferred_element_type=jnp.float32)
    for rel, out in enumerate((o0, o1, o2, o3)):
        for m in range(SIDE):
            d = jnp.where(
                cross == 0,
                ((y + m) & 3) * SIDE + ((x + rel) & 3),
                ((y + rel) & 3) * SIDE + ((x + m) & 3),
            )
            for k in range(2):
                start = pl.multiple_of(k * B + d * 8, 8)
                for t in range(3):
                    out[m, k, :, t * 256 : (t + 1) * 256] = acc[t, pl.ds(start, 8), :]


def vmem():
    return pl.BlockSpec(memory_space=pltpu.VMEM)


def smem():
    return pl.BlockSpec(memory_space=pltpu.SMEM)


def params(mib):
    return pltpu.CompilerParams(vmem_limit_bytes=mib * 2**20)


def local(a_blocks, a_cols, p_blocks, p_aggs, agglo):
    shard = p_blocks[0]
    line_f = lax.ppermute(shard, BOTH, first(1))
    line_b = lax.ppermute(shard, BOTH, first(-1))
    line_d = lax.ppermute(shard, BOTH, first(2))
    a_near, shard_near = pl.pallas_call(
        fetch_kernel,
        out_shape=[
            jax.ShapeDtypeStruct(a_blocks.shape, a_blocks.dtype),
            jax.ShapeDtypeStruct(shard.shape, shard.dtype),
        ],
        in_specs=[pl.BlockSpec(memory_space=pl.ANY)] * 2,
        out_specs=[vmem()] * 2,
        scratch_shapes=[pltpu.SemaphoreType.DMA((2,))],
        compiler_params=params(8),
        name="fetch",
    )(a_blocks, shard)
    line = jnp.concatenate([shard_near, line_f, line_d, line_b])
    plane_d = lax.ppermute(line, BOTH, second(2))
    near = lax.ppermute(line, "row", row_pairs(1))
    plane_d, near = lax.optimization_barrier((plane_d, near))
    lines = jnp.concatenate([line, near])
    plane_f = lax.ppermute(lines, BOTH, second(1))
    plane_b = lax.ppermute(lines, BOTH, second(-1))
    far = lax.ppermute(plane_d, "row", row_pairs(1))
    plane_f, plane_b, far = lax.optimization_barrier((plane_f, plane_b, far))
    plane = jnp.concatenate([line, plane_f[:8], plane_d, plane_b[:8]])
    pair = lax.ppermute(plane, "row", row_pairs(0))

    cols, aggs = a_cols.T, p_aggs.T
    split = pl.pallas_call(
        lift_kernel,
        out_shape=jax.ShapeDtypeStruct((2 * ROWS, 256, 256), jnp.bfloat16),
        in_specs=[smem(), smem(), vmem(), vmem()],
        out_specs=vmem(),
        compiler_params=params(16),
        name="lift",
    )(aggs, agglo, a_near, plane)
    piece = jax.ShapeDtypeStruct((SIDE, 2, 8, 768), jnp.float32)
    o0, o1, o2, o3 = pl.pallas_call(
        band_kernel,
        out_shape=[piece] * 4,
        in_specs=[smem()] * 3 + [vmem()] * 7,
        out_specs=[vmem()] * 4,
        scratch_shapes=[
            pltpu.VMEM((96, B, B), jnp.bfloat16),
            pltpu.VMEM((3, 256, 256), jnp.float32),
        ],
        compiler_params=params(24),
        name="bands",
    )(cols, aggs, agglo, split, plane, near, plane_f, plane_b, far, pair)

    d = lax.ppermute(o2, BOTH, first(2))
    f = lax.ppermute(o1, BOTH, first(1))
    b = lax.ppermute(o3, BOTH, first(-1))
    kept, to_f, to_d, to_b = (o0[m] + f[m] + d[m] + b[m] for m in range(SIDE))
    d = lax.ppermute(to_d, BOTH, second(2))
    f = lax.ppermute(to_f, BOTH, second(1))
    b = lax.ppermute(to_b, BOTH, second(-1))
    return (kept + f + d + b).reshape(2, 8, 6, B)


def solution(mesh):
    placed = (
        P("row", "col", None, None),
        P("row", "col"),
        P(("row", "col"), None, None, None),
        P(),
        P(),
    )
    return jax.shard_map(
        local, mesh=mesh, in_specs=placed, out_specs=P("row", "col", None, None), check_vma=False
    )
```

```python
import jax
import jax.numpy as jnp
from jax import lax
from jax.experimental import pallas as pl
from jax.experimental.pallas import tpu as pltpu
from jax.sharding import PartitionSpec as P

ROWS = 16
SIDE = 4
B = 128
BOTH = ("row", "col")


def crossed(row):
    return (row + 1) // 2 % 2


def moved(along, step):
    pairs = []
    for r in range(ROWS):
        dy, dx = ((0, step), (step, 0))[crossed(r) ^ along]
        for y in range(SIDE):
            for x in range(SIDE):
                target = ((y + dy) % SIDE) * SIDE + (x + dx) % SIDE
                pairs.append((r * ROWS + y * SIDE + x, r * ROWS + target))
    return pairs


def first(step):
    return moved(0, step)


def second(step):
    return moved(1, step)


def row_pairs(start):
    pairs = []
    for r in range(start, ROWS - 1, 2):
        pairs += [(r, r + 1), (r + 1, r)]
    return pairs


def place():
    row = lax.axis_index("row")
    col = lax.axis_index("col")
    return row, crossed(row), col // SIDE, col % SIDE


def groups_of_eight():
    groups = []
    for r in range(1, ROWS, 2):
        for q in range(SIDE):
            group = []
            for row in (r, (r + 1) % ROWS):
                for c in range(SIDE):
                    y, x = (c, q) if crossed(row) else (q, c)
                    group.append(row * ROWS + y * SIDE + x)
            groups.append(group)
    return groups


def spot_of(y, x, j, cross):
    y2, x2 = (j % ROWS) // SIDE, j % SIDE
    back = jnp.where(cross == 0, y - y2, x - x2) & 3
    return back, jnp.where(cross == 0, x2, y2)


def lift_kernel(aggs, agglo, a, plane, split):
    row, cross, y, x = place()
    for i in range(ROWS):
        swap = agglo[aggs[0, row * ROWS + i]] & 1
        back, along = spot_of(y, x, i, cross)
        spot = (back * SIDE + along) * 2
        left = jnp.concatenate([plane[spot + swap], plane[spot + 1 - swap]], axis=1)
        right = jnp.concatenate([a[i, 0], a[i, 1]], axis=1)
        lifted = lax.dot_general(
            left, right, (((0,), (0,)), ((), ())), preferred_element_type=jnp.float32
        )
        high = lifted.astype(jnp.bfloat16)
        low = (lifted - high.astype(jnp.float32)).astype(jnp.bfloat16)
        for s in range(2):
            split[i * 2 + s, :, :B] = high[:, s * B : (s + 1) * B]
            split[i * 2 + s, :, B:] = low[:, s * B : (s + 1) * B]


def band_kernel(cols, aggs, agglo, split, lines, f, b, d, far, pair, out, blocks, acc):
    row, cross, y, x = place()
    own_half = 1 - row % 2
    blocks[0:16] = lines[...]
    blocks[16:32] = f[...]
    blocks[pl.ds(32 + own_half * 8, 8)] = d[...]
    blocks[pl.ds(40 - own_half * 8, 8)] = far[...]
    blocks[48:64] = b[...]
    blocks[64:96] = pair[...]
    acc[...] = jnp.zeros_like(acc)
    pair_band = 2 - 2 * (row % 2)
    for i in range(ROWS):
        for s in range(2):
            j = cols[s, i]
            swap = agglo[aggs[0, j]] & 1
            band = j // ROWS - row + 1
            of_pair = band == pair_band
            half = jnp.where(band == 1, own_half, 1 - own_half)
            back, along = spot_of(y, x, j, jnp.where(of_pair, 1 - cross, cross))
            spot = jnp.where(
                of_pair,
                64 + (back * SIDE + along) * 2,
                back * 16 + half * 8 + along * 2,
            )
            right = jnp.concatenate([blocks[spot + swap], blocks[spot + 1 - swap]], axis=1)
            right = jnp.concatenate([right, right], axis=0)
            acc[band] += jnp.dot(split[i * 2 + s], right, preferred_element_type=jnp.float32)
    for d in range(ROWS):
        for k in range(2):
            for t in range(3):
                out[d, k, :, t * 256 : (t + 1) * 256] = acc[t, k * B + d * 8 : k * B + d * 8 + 8, :]


def vmem():
    return pl.BlockSpec(memory_space=pltpu.VMEM)


def smem():
    return pl.BlockSpec(memory_space=pltpu.SMEM)


def params(mib):
    return pltpu.CompilerParams(vmem_limit_bytes=mib * 2**20)


def local(a_blocks, a_cols, p_blocks, p_aggs, agglo):
    own = (1 - (lax.axis_index("row") & 1)) * 8

    def own_half(lines):
        return lax.dynamic_slice_in_dim(lines, own, 8, 0)

    copies = jnp.broadcast_to(p_blocks, (8, 2, B, B))
    lines = lax.all_to_all(
        copies, BOTH, 0, 0, axis_index_groups=groups_of_eight(), tiled=True
    ).reshape(16, B, B)
    line = own_half(lines)
    plane_d = lax.ppermute(line, BOTH, second(2))
    plane_f = lax.ppermute(lines, BOTH, second(1))
    plane_b = lax.ppermute(lines, BOTH, second(-1))
    far = lax.ppermute(plane_d, "row", row_pairs(1))
    plane_f, plane_b, far = lax.optimization_barrier((plane_f, plane_b, far))
    plane = jnp.concatenate([line, own_half(plane_f), plane_d, own_half(plane_b)])
    pair = lax.ppermute(plane, "row", row_pairs(0))

    cols, aggs = a_cols.T, p_aggs.T
    split = pl.pallas_call(
        lift_kernel,
        out_shape=jax.ShapeDtypeStruct((2 * ROWS, 256, 256), jnp.bfloat16),
        in_specs=[smem(), smem(), vmem(), vmem()],
        out_specs=vmem(),
        compiler_params=params(16),
        name="lift",
    )(aggs, agglo, a_blocks, plane)
    partial = pl.pallas_call(
        band_kernel,
        out_shape=jax.ShapeDtypeStruct((ROWS, 2, 8, 768), jnp.float32),
        in_specs=[smem()] * 3 + [vmem()] * 7,
        out_specs=vmem(),
        scratch_shapes=[
            pltpu.VMEM((96, B, B), jnp.bfloat16),
            pltpu.VMEM((3, 256, 256), jnp.float32),
        ],
        compiler_params=params(24),
        name="bands",
    )(cols, aggs, agglo, split, lines, plane_f, plane_b, plane_d, far, pair)
    parts = lax.all_to_all(partial, "col", 0, 0, tiled=True)
    return parts.sum(0).reshape(2, 8, 6, B)


def solution(mesh):
    placed = (
        P("row", "col", None, None),
        P("row", "col"),
        P(("row", "col"), None, None, None),
        P(),
        P(),
    )
    return jax.shard_map(
        local, mesh=mesh, in_specs=placed, out_specs=P("row", "col", None, None), check_vma=False
    )
```

```python
import jax
import jax.numpy as jnp
from jax import lax
from jax.experimental import pallas as pl
from jax.experimental.pallas import tpu as pltpu
from jax.sharding import PartitionSpec as P

ROWS = 16
SIDE = 4
B = 128
BOTH = ("row", "col")


def crossed(row):
    return (row + 1) // 2 % 2


def swapped(along, k):
    pairs = []
    for r in range(ROWS):
        dy, dx = ((0, k), (k, 0))[crossed(r) ^ along]
        for y in range(SIDE):
            for x in range(SIDE):
                pairs.append((r * ROWS + y * SIDE + x, r * ROWS + (y ^ dy) * SIDE + (x ^ dx)))
    return pairs


def first(k):
    return swapped(0, k)


def second(k):
    return swapped(1, k)


def row_pairs(start):
    pairs = []
    for r in range(start, ROWS - 1, 2):
        pairs += [(r, r + 1), (r + 1, r)]
    return pairs


def place():
    row = lax.axis_index("row")
    col = lax.axis_index("col")
    return row, crossed(row), col // SIDE, col % SIDE


def slot_of(y, x, j, cross):
    dy, dx = y ^ ((j % ROWS) // SIDE), x ^ (j % SIDE)
    return jnp.where(cross == 0, dy * SIDE + dx, dx * SIDE + dy)


def fetch_kernel(shard, near):
    near[...] = shard[...]


def lift_kernel(aggs, agglo, a, plane, split):
    row, cross, y, x = place()
    for i in range(ROWS):
        swap = agglo[aggs[0, row * ROWS + i]] & 1
        spot = slot_of(y, x, i, cross) * 2
        left = jnp.concatenate([plane[spot + swap], plane[spot + 1 - swap]], axis=1)
        right = jnp.concatenate([a[i, 0], a[i, 1]], axis=1)
        lifted = lax.dot_general(
            left, right, (((0,), (0,)), ((), ())), preferred_element_type=jnp.float32
        )
        high = lifted.astype(jnp.bfloat16)
        low = (lifted - high.astype(jnp.float32)).astype(jnp.bfloat16)
        for s in range(2):
            split[i * 2 + s, :, :B] = high[:, s * B : (s + 1) * B]
            split[i * 2 + s, :, B:] = low[:, s * B : (s + 1) * B]


def band_kernel(
    cols, aggs, agglo, split, plane, near, f, b, far, pair, o0, o1, o2, o3, blocks, acc
):
    row, cross, y, x = place()
    blocks[0:32] = plane[...]
    blocks[32:40] = near[...]
    blocks[40:48] = f[8:16]
    blocks[48:56] = far[...]
    blocks[56:64] = b[8:16]
    blocks[64:96] = pair[...]
    acc[...] = jnp.zeros_like(acc)
    pair_band = 2 - 2 * (row % 2)
    for i in range(ROWS):
        for s in range(2):
            j = cols[s, i]
            swap = agglo[aggs[0, j]] & 1
            band = j // ROWS - row + 1
            base = jnp.where(band == 1, 0, jnp.where(band == pair_band, 64, 32))
            spot = base + slot_of(y, x, j, jnp.where(band == pair_band, 1 - cross, cross)) * 2
            right = jnp.concatenate([blocks[spot + swap], blocks[spot + 1 - swap]], axis=1)
            right = jnp.concatenate([right, right], axis=0)
            acc[band] += jnp.dot(split[i * 2 + s], right, preferred_element_type=jnp.float32)
    for rel, out in enumerate((o0, o1, o2, o3)):
        for m in range(SIDE):
            d = jnp.where(
                cross == 0,
                (y ^ m) * SIDE + (x ^ rel),
                (y ^ rel) * SIDE + (x ^ m),
            )
            for k in range(2):
                start = pl.multiple_of(k * B + d * 8, 8)
                for t in range(3):
                    out[m, k, :, t * 256 : (t + 1) * 256] = acc[t, pl.ds(start, 8), :]


def vmem():
    return pl.BlockSpec(memory_space=pltpu.VMEM)


def smem():
    return pl.BlockSpec(memory_space=pltpu.SMEM)


def params(mib):
    return pltpu.CompilerParams(vmem_limit_bytes=mib * 2**20)


def local(a_blocks, a_cols, p_blocks, p_aggs, agglo):
    shard = p_blocks[0]
    line_1, line_3, line_2 = (lax.ppermute(shard, BOTH, first(k)) for k in (1, 3, 2))
    shard_near = pl.pallas_call(
        fetch_kernel,
        out_shape=jax.ShapeDtypeStruct(shard.shape, shard.dtype),
        in_specs=[vmem()],
        out_specs=vmem(),
        compiler_params=params(8),
        name="fetch",
    )(shard)
    line = jnp.concatenate([shard_near, line_1, line_2, line_3])
    plane_2 = lax.ppermute(line, BOTH, second(2))
    near = lax.ppermute(line, "row", row_pairs(1))
    plane_2, near = lax.optimization_barrier((plane_2, near))
    lines = jnp.concatenate([line, near])
    plane_1 = lax.ppermute(lines, BOTH, second(1))
    plane_3 = lax.ppermute(lines, BOTH, second(3))
    far = lax.ppermute(plane_2, "row", row_pairs(1))
    plane_1, plane_3, far = lax.optimization_barrier((plane_1, plane_3, far))
    plane = jnp.concatenate([line, plane_1[:8], plane_2, plane_3[:8]])
    pair = lax.ppermute(plane, "row", row_pairs(0))

    cols, aggs = a_cols.T, p_aggs.T
    split = pl.pallas_call(
        lift_kernel,
        out_shape=jax.ShapeDtypeStruct((2 * ROWS, 256, 256), jnp.bfloat16),
        in_specs=[smem(), smem(), vmem(), vmem()],
        out_specs=vmem(),
        compiler_params=params(16),
        name="lift",
    )(aggs, agglo, a_blocks, plane)
    piece = jax.ShapeDtypeStruct((SIDE, 2, 8, 768), jnp.float32)
    o0, o1, o2, o3 = pl.pallas_call(
        band_kernel,
        out_shape=[piece] * 4,
        in_specs=[smem()] * 3 + [vmem()] * 7,
        out_specs=[vmem()] * 4,
        scratch_shapes=[
            pltpu.VMEM((96, B, B), jnp.bfloat16),
            pltpu.VMEM((3, 256, 256), jnp.float32),
        ],
        compiler_params=params(24),
        name="bands",
    )(cols, aggs, agglo, split, plane, near, plane_1, plane_3, far, pair)

    p1, p3, p2 = (lax.ppermute(o, BOTH, first(k)) for o, k in ((o1, 1), (o3, 3), (o2, 2)))
    sums = [o0[m] + p1[m] + p2[m] + p3[m] for m in range(SIDE)]
    q1, q3, q2 = (lax.ppermute(sums[k], BOTH, second(k)) for k in (1, 3, 2))
    return (sums[0] + q1 + q2 + q3).reshape(2, 8, 6, B)


def solution(mesh):
    placed = (
        P("row", "col", None, None),
        P("row", "col"),
        P(("row", "col"), None, None, None),
        P(),
        P(),
    )
    return jax.shard_map(
        local, mesh=mesh, in_specs=placed, out_specs=P("row", "col", None, None), check_vma=False
    )
```

```python
import jax
import jax.numpy as jnp
from jax import lax
from jax.experimental import pallas as pl
from jax.experimental.pallas import tpu as pltpu
from jax.sharding import PartitionSpec as P

ROWS = 16
SIDE = 4
B = 128
BOTH = ("row", "col")


def crossed(row):
    return (row + 1) // 2 % 2


def swapped(along, k):
    pairs = []
    for r in range(ROWS):
        dy, dx = ((0, k), (k, 0))[crossed(r) ^ along]
        for y in range(SIDE):
            for x in range(SIDE):
                pairs.append((r * ROWS + y * SIDE + x, r * ROWS + (y ^ dy) * SIDE + (x ^ dx)))
    return pairs


def first(k):
    return swapped(0, k)


def second(k):
    return swapped(1, k)


def row_pairs(start):
    pairs = []
    for r in range(start, ROWS - 1, 2):
        pairs += [(r, r + 1), (r + 1, r)]
    return pairs


def place():
    row = lax.axis_index("row")
    col = lax.axis_index("col")
    return row, crossed(row), col // SIDE, col % SIDE


def slot_of(y, x, j, cross):
    dy, dx = y ^ ((j % ROWS) // SIDE), x ^ (j % SIDE)
    back, along = jnp.where(cross == 0, dy, dx), jnp.where(cross == 0, dx, dy)
    return ((back >> 1) | ((back & 1) << 1)) * SIDE + along


def fetch_kernel(shard, near):
    near[...] = shard[...]


def lift_kernel(aggs, agglo, a, plane, split):
    row, cross, y, x = place()
    for i in range(ROWS):
        swap = agglo[aggs[0, row * ROWS + i]] & 1
        spot = slot_of(y, x, i, cross) * 2
        left = jnp.concatenate([plane[spot + swap], plane[spot + 1 - swap]], axis=1)
        right = jnp.concatenate([a[i, 0], a[i, 1]], axis=1)
        lifted = lax.dot_general(
            left, right, (((0,), (0,)), ((), ())), preferred_element_type=jnp.float32
        )
        high = lifted.astype(jnp.bfloat16)
        low = (lifted - high.astype(jnp.float32)).astype(jnp.bfloat16)
        for s in range(2):
            split[i * 2 + s, :, :B] = high[:, s * B : (s + 1) * B]
            split[i * 2 + s, :, B:] = low[:, s * B : (s + 1) * B]


def band_kernel(
    cols, aggs, agglo, split, own, near, near_13, pair, o0, o1, o2, o3, blocks, acc
):
    row, cross, y, x = place()
    blocks[0:32] = own[...]
    blocks[32:48] = near[...]
    blocks[48:64] = near_13[...]
    blocks[64:96] = pair[...]
    acc[...] = jnp.zeros_like(acc)
    pair_band = 2 - 2 * (row % 2)
    for i in range(ROWS):
        for s in range(2):
            j = cols[s, i]
            swap = agglo[aggs[0, j]] & 1
            band = j // ROWS - row + 1
            base = jnp.where(band == 1, 0, jnp.where(band == pair_band, 64, 32))
            spot = base + slot_of(y, x, j, jnp.where(band == pair_band, 1 - cross, cross)) * 2
            right = jnp.concatenate([blocks[spot + swap], blocks[spot + 1 - swap]], axis=1)
            right = jnp.concatenate([right, right], axis=0)
            acc[band] += jnp.dot(split[i * 2 + s], right, preferred_element_type=jnp.float32)
    for rel, out in enumerate((o0, o1, o2, o3)):
        for m in range(SIDE):
            d = jnp.where(
                cross == 0,
                (y ^ m) * SIDE + (x ^ rel),
                (y ^ rel) * SIDE + (x ^ m),
            )
            for k in range(2):
                start = pl.multiple_of(k * B + d * 8, 8)
                for t in range(3):
                    out[m, k, :, t * 256 : (t + 1) * 256] = acc[t, pl.ds(start, 8), :]


def vmem():
    return pl.BlockSpec(memory_space=pltpu.VMEM)


def smem():
    return pl.BlockSpec(memory_space=pltpu.SMEM)


def params(mib):
    return pltpu.CompilerParams(vmem_limit_bytes=mib * 2**20)


def local(a_blocks, a_cols, p_blocks, p_aggs, agglo):
    shard = p_blocks[0]
    across = lax.ppermute(shard, BOTH, second(2))
    shard_near = pl.pallas_call(
        fetch_kernel,
        out_shape=jax.ShapeDtypeStruct(shard.shape, shard.dtype),
        in_specs=[vmem()],
        out_specs=vmem(),
        compiler_params=params(8),
        name="fetch",
    )(shard)
    duo = jnp.concatenate([shard_near, across])
    duo_1, duo_3, duo_2 = (lax.ppermute(duo, BOTH, first(k)) for k in (1, 3, 2))
    duos = (duo, duo_1, duo_2, duo_3)
    line = jnp.concatenate([d[:2] for d in duos])
    lines = jnp.concatenate([line] + [d[2:] for d in duos])
    near = lax.ppermute(lines, "row", row_pairs(1))
    own_1 = lax.ppermute(line, BOTH, second(1))
    own_3 = lax.ppermute(line, BOTH, second(3))
    near_13 = lax.ppermute(jnp.concatenate([own_1, own_3]), "row", row_pairs(1))
    own = jnp.concatenate([lines, own_1, own_3])
    pair = lax.ppermute(own, "row", row_pairs(0))

    cost = pl.CostEstimate(flops=10**6, bytes_accessed=2**12, transcendentals=0)
    cols, aggs = a_cols.T, p_aggs.T
    split = pl.pallas_call(
        lift_kernel,
        out_shape=jax.ShapeDtypeStruct((2 * ROWS, 256, 256), jnp.bfloat16),
        in_specs=[smem(), smem(), vmem(), vmem()],
        out_specs=vmem(),
        compiler_params=params(16),
        cost_estimate=cost,
        name="lift",
    )(aggs, agglo, a_blocks, own)
    piece = jax.ShapeDtypeStruct((SIDE, 2, 8, 768), jnp.float32)
    o0, o1, o2, o3 = pl.pallas_call(
        band_kernel,
        out_shape=[piece] * 4,
        in_specs=[smem()] * 3 + [vmem()] * 5,
        out_specs=[vmem()] * 4,
        scratch_shapes=[
            pltpu.VMEM((96, B, B), jnp.bfloat16),
            pltpu.VMEM((3, 256, 256), jnp.float32),
        ],
        compiler_params=params(24),
        cost_estimate=cost,
        name="bands",
    )(cols, aggs, agglo, split, own, near, near_13, pair)

    p1, p3, p2 = (lax.ppermute(o, BOTH, first(k)) for o, k in ((o1, 1), (o3, 3), (o2, 2)))
    sums = [o0[m] + p1[m] + p2[m] + p3[m] for m in range(SIDE)]
    q1, q3, q2 = (lax.ppermute(sums[k], BOTH, second(k)) for k in (1, 3, 2))
    return (sums[0] + q1 + q2 + q3).reshape(2, 8, 6, B)


def solution(mesh):
    placed = (
        P("row", "col", None, None),
        P("row", "col"),
        P(("row", "col"), None, None, None),
        P(),
        P(),
    )
    return jax.shard_map(
        local, mesh=mesh, in_specs=placed, out_specs=P("row", "col", None, None), check_vma=False
    )
```

```python
import jax
import jax.numpy as jnp
from jax import lax
from jax.experimental import pallas as pl
from jax.experimental.pallas import tpu as pltpu
from jax.sharding import PartitionSpec as P

ROWS = 16
SIDE = 4
B = 128
BOTH = ("row", "col")


def crossed(row):
    return (row + 1) // 2 % 2


def swapped(along, k):
    pairs = []
    for r in range(ROWS):
        dy, dx = ((0, k), (k, 0))[crossed(r) ^ along]
        for y in range(SIDE):
            for x in range(SIDE):
                pairs.append((r * ROWS + y * SIDE + x, r * ROWS + (y ^ dy) * SIDE + (x ^ dx)))
    return pairs


def first(k):
    return swapped(0, k)


def second(k):
    return swapped(1, k)


def row_pairs(start):
    pairs = []
    for r in range(start, ROWS - 1, 2):
        pairs += [(r, r + 1), (r + 1, r)]
    return pairs


def place():
    row = lax.axis_index("row")
    col = lax.axis_index("col")
    return row, crossed(row), col // SIDE, col % SIDE


def slot_of(y, x, j, cross):
    dy, dx = y ^ ((j % ROWS) // SIDE), x ^ (j % SIDE)
    return jnp.where(cross == 0, dy * SIDE + dx, dx * SIDE + dy)


def fetch_kernel(shard, near):
    near[...] = shard[...]


def lift_kernel(aggs, agglo, a, plane, split):
    row, cross, y, x = place()
    for i in range(ROWS):
        swap = agglo[aggs[0, row * ROWS + i]] & 1
        spot = slot_of(y, x, i, cross) * 2
        left = jnp.concatenate([plane[spot + swap], plane[spot + 1 - swap]], axis=1)
        right = jnp.concatenate([a[i, 0], a[i, 1]], axis=1)
        lifted = lax.dot_general(
            left, right, (((0,), (0,)), ((), ())), preferred_element_type=jnp.float32
        )
        high = lifted.astype(jnp.bfloat16)
        low = (lifted - high.astype(jnp.float32)).astype(jnp.bfloat16)
        for s in range(2):
            split[i * 2 + s, :, :B] = high[:, s * B : (s + 1) * B]
            split[i * 2 + s, :, B:] = low[:, s * B : (s + 1) * B]


def scatter_rows(cross, y, x, acc, outs, bands):
    for rel, out in enumerate(outs):
        for m in range(SIDE):
            d = jnp.where(
                cross == 0,
                (y ^ m) * SIDE + (x ^ rel),
                (y ^ rel) * SIDE + (x ^ m),
            )
            for k in range(2):
                start = pl.multiple_of(k * B + d * 8, 8)
                for t in range(bands):
                    out[m, k, :, t * 256 : (t + 1) * 256] = acc[t, pl.ds(start, 8), :]


def add_products(cols, aggs, agglo, split, blocks, acc, target):
    acc[...] = jnp.zeros_like(acc)
    for i in range(ROWS):
        for s in range(2):
            j = cols[s, i]
            swap = agglo[aggs[0, j]] & 1
            t, spot = target(j)
            right = jnp.concatenate([blocks[spot + swap], blocks[spot + 1 - swap]], axis=1)
            right = jnp.concatenate([right, right], axis=0)
            acc[t] += jnp.dot(split[i * 2 + s], right, preferred_element_type=jnp.float32)


def home_kernel(cols, aggs, agglo, split, own, pair, o0, o1, o2, o3, blocks, acc):
    row, cross, y, x = place()
    blocks[0:32] = own[...]
    blocks[32:64] = pair[...]
    pair_band = 2 - 2 * (row % 2)

    def target(j):
        band = j // ROWS - row + 1
        of_pair = band == pair_band
        spot = slot_of(y, x, j, jnp.where(of_pair, 1 - cross, cross)) * 2
        t = jnp.where(band == 1, 0, jnp.where(of_pair, 1, 2))
        return t, jnp.where(of_pair, 32, 0) + spot

    add_products(cols, aggs, agglo, split, blocks, acc, target)
    scatter_rows(cross, y, x, acc, (o0, o1, o2, o3), 2)


def beside_kernel(cols, aggs, agglo, split, near, near_rest, o0, o1, o2, o3, blocks, acc):
    row, cross, y, x = place()
    blocks[0:8] = near[...]
    blocks[8:32] = near_rest[...]
    band_beside = 2 * (row % 2)

    def target(j):
        t = jnp.where(j // ROWS - row + 1 == band_beside, 0, 1)
        return t, slot_of(y, x, j, cross) * 2

    add_products(cols, aggs, agglo, split, blocks, acc, target)
    scatter_rows(cross, y, x, acc, (o0, o1, o2, o3), 1)


def vmem():
    return pl.BlockSpec(memory_space=pltpu.VMEM)


def smem():
    return pl.BlockSpec(memory_space=pltpu.SMEM)


def params(mib):
    return pltpu.CompilerParams(vmem_limit_bytes=mib * 2**20)


def local(a_blocks, a_cols, p_blocks, p_aggs, agglo):
    shard = p_blocks[0]
    line_1, line_3, line_2 = (lax.ppermute(shard, BOTH, first(k)) for k in (1, 3, 2))
    shard_near = pl.pallas_call(
        fetch_kernel,
        out_shape=jax.ShapeDtypeStruct(shard.shape, shard.dtype),
        in_specs=[vmem()],
        out_specs=vmem(),
        compiler_params=params(8),
        name="fetch",
    )(shard)
    line = jnp.concatenate([shard_near, line_1, line_2, line_3])
    near = lax.ppermute(line, "row", row_pairs(1))
    own_1, own_3, own_2 = (lax.ppermute(line, BOTH, second(k)) for k in (1, 3, 2))
    near, own_1, own_2, own_3 = lax.optimization_barrier((near, own_1, own_2, own_3))
    near_rest = lax.ppermute(jnp.concatenate([own_1, own_2, own_3]), "row", row_pairs(1))
    own = jnp.concatenate([line, own_1, own_2, own_3])
    pair = lax.ppermute(own, "row", row_pairs(0))

    cols, aggs = a_cols.T, p_aggs.T
    cost = pl.CostEstimate(flops=10**6, bytes_accessed=2**12, transcendentals=0)
    split = pl.pallas_call(
        lift_kernel,
        out_shape=jax.ShapeDtypeStruct((2 * ROWS, 256, 256), jnp.bfloat16),
        in_specs=[smem(), smem(), vmem(), vmem()],
        out_specs=vmem(),
        compiler_params=params(16),
        cost_estimate=cost,
        name="lift",
    )(aggs, agglo, a_blocks, own)

    def partial_sums(kernel, name, width, slots, bands, *planes):
        return pl.pallas_call(
            kernel,
            out_shape=[jax.ShapeDtypeStruct((SIDE, 2, 8, width), jnp.float32)] * SIDE,
            in_specs=[smem()] * 3 + [vmem()] * 3,
            out_specs=[vmem()] * SIDE,
            scratch_shapes=[
                pltpu.VMEM((slots, B, B), jnp.bfloat16),
                pltpu.VMEM((bands, 256, 256), jnp.float32),
            ],
            compiler_params=params(16),
            cost_estimate=cost,
            name=name,
        )(cols, aggs, agglo, split, *planes)

    def reduced(o0, o1, o2, o3):
        p1, p3, p2 = (lax.ppermute(o, BOTH, first(k)) for o, k in ((o1, 1), (o3, 3), (o2, 2)))
        return o0, p1, p2, p3

    home = reduced(*partial_sums(home_kernel, "home", 512, 64, 3, own, pair))
    *home, near_rest = lax.optimization_barrier((*home, near_rest))
    beside = reduced(*partial_sums(beside_kernel, "beside", 256, 32, 2, near, near_rest))
    even = (lax.axis_index("row") & 1) == 0

    def ordered(m):
        mine, side = (sum(p[m] for p in parts) for parts in (home, beside))
        centre, partner = mine[..., :256], mine[..., 256:]
        low, high = jnp.where(even, side, partner), jnp.where(even, partner, side)
        return jnp.concatenate([low, centre, high], axis=-1)

    sums = [ordered(m) for m in range(SIDE)]
    q1, q3, q2 = (lax.ppermute(sums[k], BOTH, second(k)) for k in (1, 3, 2))
    return (sums[0] + q1 + q2 + q3).reshape(2, 8, 6, B)


def solution(mesh):
    placed = (
        P("row", "col", None, None),
        P("row", "col"),
        P(("row", "col"), None, None, None),
        P(),
        P(),
    )
    return jax.shard_map(
        local, mesh=mesh, in_specs=placed, out_specs=P("row", "col", None, None), check_vma=False
    )
```

```python
import jax
import jax.numpy as jnp
from jax import lax
from jax.experimental import pallas as pl
from jax.experimental.pallas import tpu as pltpu
from jax.sharding import PartitionSpec as P

ROWS = 16
SIDE = 4
B = 128
BOTH = ("row", "col")


def crossed(row):
    return (row + 1) // 2 % 2


def swapped(along, k):
    pairs = []
    for r in range(ROWS):
        dy, dx = ((0, k), (k, 0))[crossed(r) ^ along]
        for y in range(SIDE):
            for x in range(SIDE):
                pairs.append((r * ROWS + y * SIDE + x, r * ROWS + (y ^ dy) * SIDE + (x ^ dx)))
    return pairs


def first(k):
    return swapped(0, k)


def second(k):
    return swapped(1, k)


def row_pairs(start):
    pairs = []
    for r in range(start, ROWS - 1, 2):
        pairs += [(r, r + 1), (r + 1, r)]
    return pairs


def place():
    row = lax.axis_index("row")
    col = lax.axis_index("col")
    return row, crossed(row), col // SIDE, col % SIDE


def slot_of(y, x, j, cross):
    dy, dx = y ^ ((j % ROWS) // SIDE), x ^ (j % SIDE)
    back, along = jnp.where(cross == 0, dy, dx), jnp.where(cross == 0, dx, dy)
    return ((back >> 1) | ((back & 1) << 1)) * SIDE + along


def fetch_kernel(shard, near):
    near[...] = shard[...]


def lift_kernel(aggs, agglo, a, plane, split):
    row, cross, y, x = place()
    for i in range(ROWS):
        swap = agglo[aggs[0, row * ROWS + i]] & 1
        spot = slot_of(y, x, i, cross) * 2
        left = jnp.concatenate([plane[spot + swap], plane[spot + 1 - swap]], axis=1)
        right = jnp.concatenate([a[i, 0], a[i, 1]], axis=1)
        lifted = lax.dot_general(
            left, right, (((0,), (0,)), ((), ())), preferred_element_type=jnp.float32
        )
        high = lifted.astype(jnp.bfloat16)
        low = (lifted - high.astype(jnp.float32)).astype(jnp.bfloat16)
        for s in range(2):
            split[i * 2 + s, :, :B] = high[:, s * B : (s + 1) * B]
            split[i * 2 + s, :, B:] = low[:, s * B : (s + 1) * B]


def band_kernel(
    cols, aggs, agglo, split, own, near, near_2, f, b, pair, pair_rest, o0, o1, o2, o3, blocks, acc
):
    row, cross, y, x = place()
    blocks[0:32] = own[...]
    blocks[32:40] = near[...]
    blocks[40:48] = near_2[...]
    blocks[48:56] = f[8:16]
    blocks[56:64] = b[8:16]
    blocks[64:80] = pair[...]
    blocks[80:96] = pair_rest[...]
    acc[...] = jnp.zeros_like(acc)
    pair_band = 2 - 2 * (row % 2)
    for i in range(ROWS):
        for s in range(2):
            j = cols[s, i]
            swap = agglo[aggs[0, j]] & 1
            band = j // ROWS - row + 1
            base = jnp.where(band == 1, 0, jnp.where(band == pair_band, 64, 32))
            spot = base + slot_of(y, x, j, jnp.where(band == pair_band, 1 - cross, cross)) * 2
            right = jnp.concatenate([blocks[spot + swap], blocks[spot + 1 - swap]], axis=1)
            right = jnp.concatenate([right, right], axis=0)
            acc[band] += jnp.dot(split[i * 2 + s], right, preferred_element_type=jnp.float32)
    for rel, out in enumerate((o0, o1, o2, o3)):
        for m in range(SIDE):
            d = jnp.where(
                cross == 0,
                (y ^ m) * SIDE + (x ^ rel),
                (y ^ rel) * SIDE + (x ^ m),
            )
            for k in range(2):
                start = pl.multiple_of(k * B + d * 8, 8)
                for t in range(3):
                    out[m, k, :, t * 256 : (t + 1) * 256] = acc[t, pl.ds(start, 8), :]


def vmem():
    return pl.BlockSpec(memory_space=pltpu.VMEM)


def smem():
    return pl.BlockSpec(memory_space=pltpu.SMEM)


def params(mib):
    return pltpu.CompilerParams(vmem_limit_bytes=mib * 2**20)


def local(a_blocks, a_cols, p_blocks, p_aggs, agglo):
    shard = p_blocks[0]
    across = lax.ppermute(shard, BOTH, second(2))
    beside = lax.ppermute(shard, "row", row_pairs(1))
    shard_near = pl.pallas_call(
        fetch_kernel,
        out_shape=jax.ShapeDtypeStruct(shard.shape, shard.dtype),
        in_specs=[vmem()],
        out_specs=vmem(),
        compiler_params=params(8),
        name="fetch",
    )(shard)
    trio = jnp.concatenate([shard_near, across, beside])
    trio_1, trio_3, trio_2 = (lax.ppermute(trio, BOTH, first(k)) for k in (1, 3, 2))
    line, line_2, near = (
        jnp.concatenate([t[2 * n : 2 * n + 2] for t in (trio, trio_1, trio_2, trio_3)])
        for n in range(3)
    )
    lines = jnp.concatenate([line, near])
    lines_1 = lax.ppermute(lines, BOTH, second(1))
    lines_3 = lax.ppermute(lines, BOTH, second(3))
    near_2 = lax.ppermute(line_2, "row", row_pairs(1))
    home = jnp.concatenate([line, line_2])
    pair = lax.ppermute(home, "row", row_pairs(0))
    lines_1, lines_3, near_2, pair = lax.optimization_barrier((lines_1, lines_3, near_2, pair))
    rest = jnp.concatenate([lines_1[:8], lines_3[:8]])
    pair_rest = lax.ppermute(rest, "row", row_pairs(0))
    own = jnp.concatenate([home, rest])

    cols, aggs = a_cols.T, p_aggs.T
    split = pl.pallas_call(
        lift_kernel,
        out_shape=jax.ShapeDtypeStruct((2 * ROWS, 256, 256), jnp.bfloat16),
        in_specs=[smem(), smem(), vmem(), vmem()],
        out_specs=vmem(),
        compiler_params=params(16),
        name="lift",
    )(aggs, agglo, a_blocks, own)
    piece = jax.ShapeDtypeStruct((SIDE, 2, 8, 768), jnp.float32)
    o0, o1, o2, o3 = pl.pallas_call(
        band_kernel,
        out_shape=[piece] * 4,
        in_specs=[smem()] * 3 + [vmem()] * 8,
        out_specs=[vmem()] * 4,
        scratch_shapes=[
            pltpu.VMEM((96, B, B), jnp.bfloat16),
            pltpu.VMEM((3, 256, 256), jnp.float32),
        ],
        compiler_params=params(24),
        name="bands",
    )(cols, aggs, agglo, split, own, near, near_2, lines_1, lines_3, pair, pair_rest)

    p1, p3, p2 = (lax.ppermute(o, BOTH, first(k)) for o, k in ((o1, 1), (o3, 3), (o2, 2)))
    sums = [o0[m] + p1[m] + p2[m] + p3[m] for m in range(SIDE)]
    q1, q3, q2 = (lax.ppermute(sums[k], BOTH, second(k)) for k in (1, 3, 2))
    return (sums[0] + q1 + q2 + q3).reshape(2, 8, 6, B)


def solution(mesh):
    placed = (
        P("row", "col", None, None),
        P("row", "col"),
        P(("row", "col"), None, None, None),
        P(),
        P(),
    )
    return jax.shard_map(
        local, mesh=mesh, in_specs=placed, out_specs=P("row", "col", None, None), check_vma=False
    )
```

```python
import jax
import jax.numpy as jnp
from jax import lax
from jax.experimental import pallas as pl
from jax.experimental.pallas import tpu as pltpu
from jax.sharding import PartitionSpec as P

ROWS = 16
SIDE = 4
B = 128
BOTH = ("row", "col")


def crossed(row):
    return (row + 1) // 2 % 2


def swapped(along, k):
    pairs = []
    for r in range(ROWS):
        dy, dx = ((0, k), (k, 0))[crossed(r) ^ along]
        for y in range(SIDE):
            for x in range(SIDE):
                pairs.append((r * ROWS + y * SIDE + x, r * ROWS + (y ^ dy) * SIDE + (x ^ dx)))
    return pairs


def first(k):
    return swapped(0, k)


def second(k):
    return swapped(1, k)


def row_pairs(start):
    pairs = []
    for r in range(start, ROWS - 1, 2):
        pairs += [(r, r + 1), (r + 1, r)]
    return pairs


def place():
    row = lax.axis_index("row")
    col = lax.axis_index("col")
    return row, crossed(row), col // SIDE, col % SIDE


def groups_of_eight():
    groups = []
    for r in range(1, ROWS, 2):
        for q in range(SIDE):
            group = []
            for row in (r, (r + 1) % ROWS):
                for c in range(SIDE):
                    y, x = (c, q) if crossed(row) else (q, c)
                    group.append(row * ROWS + y * SIDE + x)
            groups.append(group)
    return groups


def slot_of(y, x, j, cross):
    y2, x2 = (j % ROWS) // SIDE, j % SIDE
    back, along = jnp.where(cross == 0, y ^ y2, x ^ x2), jnp.where(cross == 0, x2, y2)
    return ((back >> 1) | ((back & 1) << 1)) * SIDE + along


def spread_kernel(shard, copies, sems):
    sent = [pltpu.make_async_copy(shard, copies.at[pl.ds(n, 1)], sems.at[n]) for n in range(8)]
    for copy in sent:
        copy.start()
    for copy in sent:
        copy.wait()


def lift_kernel(aggs, agglo, a, plane, split):
    row, cross, y, x = place()
    for i in range(ROWS):
        swap = agglo[aggs[0, row * ROWS + i]] & 1
        spot = slot_of(y, x, i, cross) * 2
        left = jnp.concatenate([plane[spot + swap], plane[spot + 1 - swap]], axis=1)
        right = jnp.concatenate([a[i, 0], a[i, 1]], axis=1)
        lifted = lax.dot_general(
            left, right, (((0,), (0,)), ((), ())), preferred_element_type=jnp.float32
        )
        high = lifted.astype(jnp.bfloat16)
        low = (lifted - high.astype(jnp.float32)).astype(jnp.bfloat16)
        for s in range(2):
            split[i * 2 + s, :, :B] = high[:, s * B : (s + 1) * B]
            split[i * 2 + s, :, B:] = low[:, s * B : (s + 1) * B]


def band_kernel(
    cols, aggs, agglo, split, own, lines, near_2, f, b, pair, pair_rest, o0, o1, o2, o3, blocks, acc
):
    row, cross, y, x = place()
    other = pl.ds((row % 2) * 8, 8)
    blocks[0:32] = own[...]
    blocks[32:40] = lines[other]
    blocks[40:48] = near_2[...]
    blocks[48:56] = f[other]
    blocks[56:64] = b[other]
    blocks[64:80] = pair[...]
    blocks[80:96] = pair_rest[...]
    acc[...] = jnp.zeros_like(acc)
    pair_band = 2 - 2 * (row % 2)
    for i in range(ROWS):
        for s in range(2):
            j = cols[s, i]
            swap = agglo[aggs[0, j]] & 1
            band = j // ROWS - row + 1
            base = jnp.where(band == 1, 0, jnp.where(band == pair_band, 64, 32))
            spot = base + slot_of(y, x, j, jnp.where(band == pair_band, 1 - cross, cross)) * 2
            right = jnp.concatenate([blocks[spot + swap], blocks[spot + 1 - swap]], axis=1)
            right = jnp.concatenate([right, right], axis=0)
            acc[band] += jnp.dot(split[i * 2 + s], right, preferred_element_type=jnp.float32)
    for rel, out in enumerate((o0, o1, o2, o3)):
        for m in range(SIDE):
            d = jnp.where(
                cross == 0,
                (y ^ m) * SIDE + (x ^ rel),
                (y ^ rel) * SIDE + (x ^ m),
            )
            for k in range(2):
                start = pl.multiple_of(k * B + d * 8, 8)
                for t in range(3):
                    out[m, k, :, t * 256 : (t + 1) * 256] = acc[t, pl.ds(start, 8), :]


def vmem():
    return pl.BlockSpec(memory_space=pltpu.VMEM)


def smem():
    return pl.BlockSpec(memory_space=pltpu.SMEM)


def params(mib):
    return pltpu.CompilerParams(vmem_limit_bytes=mib * 2**20)


def local(a_blocks, a_cols, p_blocks, p_aggs, agglo):
    half = (1 - (lax.axis_index("row") & 1)) * 8

    def own_half(lines):
        return lax.dynamic_slice_in_dim(lines, half, 8, 0)

    copies = pl.pallas_call(
        spread_kernel,
        out_shape=jax.ShapeDtypeStruct((8, 2, B, B), jnp.bfloat16),
        in_specs=[pl.BlockSpec(memory_space=pltpu.HBM)],
        out_specs=pl.BlockSpec(memory_space=pltpu.HBM),
        scratch_shapes=[pltpu.SemaphoreType.DMA((8,))],
        compiler_params=params(8),
        name="spread",
    )(p_blocks)
    lines = lax.all_to_all(
        copies, BOTH, 0, 0, axis_index_groups=groups_of_eight(), tiled=True
    ).reshape(16, B, B)
    line = own_half(lines)
    line_2 = lax.ppermute(line, BOTH, second(2))
    lines_1 = lax.ppermute(lines, BOTH, second(1))
    lines_3 = lax.ppermute(lines, BOTH, second(3))
    near_2 = lax.ppermute(line_2, "row", row_pairs(1))
    home = jnp.concatenate([line, line_2])
    pair = lax.ppermute(home, "row", row_pairs(0))
    lines_1, lines_3, near_2, pair = lax.optimization_barrier((lines_1, lines_3, near_2, pair))
    rest = jnp.concatenate([own_half(lines_1), own_half(lines_3)])
    pair_rest = lax.ppermute(rest, "row", row_pairs(0))
    own = jnp.concatenate([home, rest])

    cols, aggs = a_cols.T, p_aggs.T
    split = pl.pallas_call(
        lift_kernel,
        out_shape=jax.ShapeDtypeStruct((2 * ROWS, 256, 256), jnp.bfloat16),
        in_specs=[smem(), smem(), vmem(), vmem()],
        out_specs=vmem(),
        compiler_params=params(16),
        name="lift",
    )(aggs, agglo, a_blocks, own)
    piece = jax.ShapeDtypeStruct((SIDE, 2, 8, 768), jnp.float32)
    o0, o1, o2, o3 = pl.pallas_call(
        band_kernel,
        out_shape=[piece] * 4,
        in_specs=[smem()] * 3 + [vmem()] * 8,
        out_specs=[vmem()] * 4,
        scratch_shapes=[
            pltpu.VMEM((96, B, B), jnp.bfloat16),
            pltpu.VMEM((3, 256, 256), jnp.float32),
        ],
        compiler_params=params(24),
        name="bands",
    )(cols, aggs, agglo, split, own, lines, near_2, lines_1, lines_3, pair, pair_rest)

    p1, p3, p2 = (lax.ppermute(o, BOTH, first(k)) for o, k in ((o1, 1), (o3, 3), (o2, 2)))
    sums = [o0[m] + p1[m] + p2[m] + p3[m] for m in range(SIDE)]
    q1, q3, q2 = (lax.ppermute(sums[k], BOTH, second(k)) for k in (1, 3, 2))
    return (sums[0] + q1 + q2 + q3).reshape(2, 8, 6, B)


def solution(mesh):
    placed = (
        P("row", "col", None, None),
        P("row", "col"),
        P(("row", "col"), None, None, None),
        P(),
        P(),
    )
    return jax.shard_map(
        local, mesh=mesh, in_specs=placed, out_specs=P("row", "col", None, None), check_vma=False
    )
```

```python
import jax
import jax.numpy as jnp
from jax import lax
from jax.experimental import pallas as pl
from jax.experimental.pallas import tpu as pltpu
from jax.sharding import PartitionSpec as P

ROWS = 16
SIDE = 4
B = 128
BOTH = ("row", "col")


def crossed(row):
    return (row + 1) // 2 % 2


def moved(along, move):
    pairs = []
    for r in range(ROWS):
        on_y = crossed(r) ^ along
        for y in range(SIDE):
            for x in range(SIDE):
                to = (move(y), x) if on_y else (y, move(x))
                pairs.append((r * ROWS + y * SIDE + x, r * ROWS + to[0] * SIDE + to[1]))
    return pairs


def shift(step):
    return moved(0, lambda c: (c + step) % SIDE)


def swap(k):
    return moved(1, lambda c: c ^ k)


def row_pairs(start):
    pairs = []
    for r in range(start, ROWS - 1, 2):
        pairs += [(r, r + 1), (r + 1, r)]
    return pairs


def place():
    row = lax.axis_index("row")
    col = lax.axis_index("col")
    return row, crossed(row), col // SIDE, col % SIDE


def slot_of(y, x, j, cross):
    y2, x2 = (j % ROWS) // SIDE, j % SIDE
    back = jnp.where(cross == 0, y ^ y2, x ^ x2)
    along = jnp.where(cross == 0, x - x2, y - y2) & 3
    return ((back >> 1) | ((back & 1) << 1)) * SIDE + along


def fetch_kernel(shard, near):
    near[...] = shard[...]


def lift_kernel(aggs, agglo, a, plane, split):
    row, cross, y, x = place()
    for i in range(ROWS):
        swap = agglo[aggs[0, row * ROWS + i]] & 1
        spot = slot_of(y, x, i, cross) * 2
        left = jnp.concatenate([plane[spot + swap], plane[spot + 1 - swap]], axis=1)
        right = jnp.concatenate([a[i, 0], a[i, 1]], axis=1)
        lifted = lax.dot_general(
            left, right, (((0,), (0,)), ((), ())), preferred_element_type=jnp.float32
        )
        high = lifted.astype(jnp.bfloat16)
        low = (lifted - high.astype(jnp.float32)).astype(jnp.bfloat16)
        for s in range(2):
            split[i * 2 + s, :, :B] = high[:, s * B : (s + 1) * B]
            split[i * 2 + s, :, B:] = low[:, s * B : (s + 1) * B]


def band_kernel(
    cols, aggs, agglo, split, own, near, near_2, f, b, pair, pair_rest, o0, o1, o2, o3, blocks, acc
):
    row, cross, y, x = place()
    blocks[0:32] = own[...]
    blocks[32:40] = near[...]
    blocks[40:48] = near_2[...]
    blocks[48:56] = f[8:16]
    blocks[56:64] = b[8:16]
    blocks[64:80] = pair[...]
    blocks[80:96] = pair_rest[...]
    acc[...] = jnp.zeros_like(acc)
    pair_band = 2 - 2 * (row % 2)
    for i in range(ROWS):
        for s in range(2):
            j = cols[s, i]
            swap = agglo[aggs[0, j]] & 1
            band = j // ROWS - row + 1
            base = jnp.where(band == 1, 0, jnp.where(band == pair_band, 64, 32))
            spot = base + slot_of(y, x, j, jnp.where(band == pair_band, 1 - cross, cross)) * 2
            right = jnp.concatenate([blocks[spot + swap], blocks[spot + 1 - swap]], axis=1)
            right = jnp.concatenate([right, right], axis=0)
            acc[band] += jnp.dot(split[i * 2 + s], right, preferred_element_type=jnp.float32)
    for rel, out in enumerate((o0, o1, o2, o3)):
        for m, back in enumerate((0, 1, 3, 2)):
            d = jnp.where(
                cross == 0,
                (y ^ back) * SIDE + ((x + rel) & 3),
                ((y + rel) & 3) * SIDE + (x ^ back),
            )
            for k in range(2):
                start = pl.multiple_of(k * B + d * 8, 8)
                for t in range(3):
                    out[m, k, :, t * 256 : (t + 1) * 256] = acc[t, pl.ds(start, 8), :]


def vmem():
    return pl.BlockSpec(memory_space=pltpu.VMEM)


def smem():
    return pl.BlockSpec(memory_space=pltpu.SMEM)


def params(mib):
    return pltpu.CompilerParams(vmem_limit_bytes=mib * 2**20)


def local(a_blocks, a_cols, p_blocks, p_aggs, agglo):
    shard = p_blocks[0]
    across = lax.ppermute(shard, BOTH, swap(2))
    beside = lax.ppermute(shard, "row", row_pairs(1))
    shard_near = pl.pallas_call(
        fetch_kernel,
        out_shape=jax.ShapeDtypeStruct(shard.shape, shard.dtype),
        in_specs=[vmem()],
        out_specs=vmem(),
        compiler_params=params(8),
        name="fetch",
    )(shard)
    trio = jnp.concatenate([shard_near, across, beside])
    trio_1, trio_3, trio_2 = (lax.ppermute(trio, BOTH, shift(k)) for k in (1, 3, 2))
    line, line_2, near = (
        jnp.concatenate([t[2 * n : 2 * n + 2] for t in (trio, trio_1, trio_2, trio_3)])
        for n in range(3)
    )
    lines = jnp.concatenate([line, near])
    lines_1 = lax.ppermute(lines, BOTH, swap(1))
    lines_3 = lax.ppermute(lines, BOTH, swap(3))
    near_2 = lax.ppermute(line_2, "row", row_pairs(1))
    home = jnp.concatenate([line, line_2])
    pair = lax.ppermute(home, "row", row_pairs(0))
    lines_1, lines_3, near_2, pair = lax.optimization_barrier((lines_1, lines_3, near_2, pair))
    rest = jnp.concatenate([lines_1[:8], lines_3[:8]])
    pair_rest = lax.ppermute(rest, "row", row_pairs(0))
    own = jnp.concatenate([home, rest])

    cols, aggs = a_cols.T, p_aggs.T
    split = pl.pallas_call(
        lift_kernel,
        out_shape=jax.ShapeDtypeStruct((2 * ROWS, 256, 256), jnp.bfloat16),
        in_specs=[smem(), smem(), vmem(), vmem()],
        out_specs=vmem(),
        compiler_params=params(16),
        name="lift",
    )(aggs, agglo, a_blocks, own)
    piece = jax.ShapeDtypeStruct((SIDE, 2, 8, 768), jnp.float32)
    o0, o1, o2, o3 = pl.pallas_call(
        band_kernel,
        out_shape=[piece] * 4,
        in_specs=[smem()] * 3 + [vmem()] * 8,
        out_specs=[vmem()] * 4,
        scratch_shapes=[
            pltpu.VMEM((96, B, B), jnp.bfloat16),
            pltpu.VMEM((3, 256, 256), jnp.float32),
        ],
        compiler_params=params(24),
        name="bands",
    )(cols, aggs, agglo, split, own, near, near_2, lines_1, lines_3, pair, pair_rest)

    p2 = lax.ppermute(o2, BOTH, shift(2))
    p1 = lax.ppermute(o1, BOTH, shift(1))
    p3 = lax.ppermute(o3, BOTH, shift(3))
    kept, sent = (o0[h] + p1[h] + p3[h] + p2[h] for h in (slice(0, 2), slice(2, 4)))
    kept = kept + lax.ppermute(sent, BOTH, swap(3))
    return (kept[0] + lax.ppermute(kept[1], BOTH, swap(1))).reshape(2, 8, 6, B)


def solution(mesh):
    placed = (
        P("row", "col", None, None),
        P("row", "col"),
        P(("row", "col"), None, None, None),
        P(),
        P(),
    )
    return jax.shard_map(
        local, mesh=mesh, in_specs=placed, out_specs=P("row", "col", None, None), check_vma=False
    )
```

```python
import functools

import jax
import jax.numpy as jnp
from jax import lax
from jax.experimental import pallas as pl
from jax.experimental.pallas import tpu as pltpu
from jax.sharding import PartitionSpec as P

ROWS = 16
SIDE = 4
B = 128
BOTH = ("row", "col")


def crossed(row):
    return (row + 1) // 2 % 2


def moved(along, move):
    pairs = []
    for r in range(ROWS):
        on_y = crossed(r) ^ along
        for y in range(SIDE):
            for x in range(SIDE):
                to = (move(y), x) if on_y else (y, move(x))
                pairs.append((r * ROWS + y * SIDE + x, r * ROWS + to[0] * SIDE + to[1]))
    return pairs


def shift(step, along=0):
    return moved(along, lambda c: (c + step) % SIDE)


def swap(k):
    return moved(1, lambda c: c ^ k)


def row_pairs(start):
    pairs = []
    for r in range(start, ROWS - 1, 2):
        pairs += [(r, r + 1), (r + 1, r)]
    return pairs


def place():
    row = lax.axis_index("row")
    col = lax.axis_index("col")
    return row, crossed(row), col // SIDE, col % SIDE


def slot_of(y, x, j, cross):
    y2, x2 = (j % ROWS) // SIDE, j % SIDE
    back = jnp.where(cross == 0, y ^ y2, x ^ x2)
    along = jnp.where(cross == 0, x - x2, y - y2) & 3
    return ((back >> 1) | ((back & 1) << 1)) * SIDE + along


def fetch_kernel(shard, near):
    near[...] = shard[...]


def row_at(y, x, slot, cross):
    back, along = (0, 2, 1, 3)[slot // SIDE], slot % SIDE
    y2 = jnp.where(cross == 0, y ^ back, (y - along) & 3)
    x2 = jnp.where(cross == 0, (x - along) & 3, x ^ back)
    return y2 * SIDE + x2


def lift_kernel(first_slot, aggs, agglo, a, blocks, split):
    row, cross, y, x = place()
    for p in range(ROWS // 2):
        i = row_at(y, x, first_slot + p, cross)
        swap = agglo[aggs[0, row * ROWS + i]] & 1
        left = jnp.concatenate([blocks[p * 2 + swap], blocks[p * 2 + 1 - swap]], axis=1)
        right = jnp.concatenate([a[i, 0], a[i, 1]], axis=1)
        lifted = lax.dot_general(
            left, right, (((0,), (0,)), ((), ())), preferred_element_type=jnp.float32
        )
        high = lifted.astype(jnp.bfloat16)
        low = (lifted - high.astype(jnp.float32)).astype(jnp.bfloat16)
        for s in range(2):
            split[p * 2 + s, :, :B] = high[:, s * B : (s + 1) * B]
            split[p * 2 + s, :, B:] = low[:, s * B : (s + 1) * B]


def band_kernel(
    cols, aggs, agglo, split, split_rest, home, rest, near, near_2, f, b, pair, pair_rest,
    o0, o1, o2, o3, blocks, acc
):
    row, cross, y, x = place()
    blocks[0:16] = home[...]
    blocks[16:32] = rest[...]
    blocks[32:40] = near[...]
    blocks[40:48] = near_2[...]
    blocks[48:56] = f[8:16]
    blocks[56:64] = b[8:16]
    blocks[64:80] = pair[...]
    blocks[80:96] = pair_rest[...]
    acc[...] = jnp.zeros_like(acc)
    pair_band = 2 - 2 * (row % 2)
    for p in range(ROWS):
        i = row_at(y, x, p, cross)
        part = split if p < ROWS // 2 else split_rest
        for s in range(2):
            j = cols[s, i]
            swap = agglo[aggs[0, j]] & 1
            band = j // ROWS - row + 1
            base = jnp.where(band == 1, 0, jnp.where(band == pair_band, 64, 32))
            spot = base + slot_of(y, x, j, jnp.where(band == pair_band, 1 - cross, cross)) * 2
            right = jnp.concatenate([blocks[spot + swap], blocks[spot + 1 - swap]], axis=1)
            right = jnp.concatenate([right, right], axis=0)
            acc[band] += jnp.dot(part[p % 8 * 2 + s], right, preferred_element_type=jnp.float32)
    for rel, out in enumerate((o0, o1, o2, o3)):
        for m in range(SIDE):
            d = jnp.where(
                cross == 0,
                ((y + m) & 3) * SIDE + ((x + rel) & 3),
                ((y + rel) & 3) * SIDE + ((x + m) & 3),
            )
            for k in range(2):
                start = pl.multiple_of(k * B + d * 8, 8)
                for t in range(3):
                    out[m, k, :, t * 256 : (t + 1) * 256] = acc[t, pl.ds(start, 8), :]


def vmem():
    return pl.BlockSpec(memory_space=pltpu.VMEM)


def smem():
    return pl.BlockSpec(memory_space=pltpu.SMEM)


def params(mib):
    return pltpu.CompilerParams(vmem_limit_bytes=mib * 2**20)


def local(a_blocks, a_cols, p_blocks, p_aggs, agglo):
    shard = p_blocks[0]
    across = lax.ppermute(shard, BOTH, swap(2))
    beside = lax.ppermute(shard, "row", row_pairs(1))
    shard_near = pl.pallas_call(
        fetch_kernel,
        out_shape=jax.ShapeDtypeStruct(shard.shape, shard.dtype),
        in_specs=[vmem()],
        out_specs=vmem(),
        compiler_params=params(8),
        name="fetch",
    )(shard)
    trio = jnp.concatenate([shard_near, across, beside])
    trio_1, trio_3, trio_2 = (lax.ppermute(trio, BOTH, shift(k)) for k in (1, 3, 2))
    line, line_2, near = (
        jnp.concatenate([t[2 * n : 2 * n + 2] for t in (trio, trio_1, trio_2, trio_3)])
        for n in range(3)
    )
    lines = jnp.concatenate([line, near])
    lines_1 = lax.ppermute(lines, BOTH, swap(1))
    lines_3 = lax.ppermute(lines, BOTH, swap(3))
    near_2 = lax.ppermute(line_2, "row", row_pairs(1))
    home = jnp.concatenate([line, line_2])
    pair = lax.ppermute(home, "row", row_pairs(0))
    cols, aggs = a_cols.T, p_aggs.T

    def lift(first_slot, blocks, name):
        return pl.pallas_call(
            functools.partial(lift_kernel, first_slot),
            out_shape=jax.ShapeDtypeStruct((ROWS, 256, 256), jnp.bfloat16),
            in_specs=[smem(), smem(), vmem(), vmem()],
            out_specs=vmem(),
            compiler_params=params(16),
            name=name,
        )(aggs, agglo, a_blocks, blocks)

    split = lift(0, home, "lift_home")
    lines_1, lines_3, near_2, pair, split = lax.optimization_barrier(
        (lines_1, lines_3, near_2, pair, split)
    )
    rest = jnp.concatenate([lines_1[:8], lines_3[:8]])
    pair_rest = lax.ppermute(rest, "row", row_pairs(0))
    split_rest = lift(ROWS // 2, rest, "lift_rest")
    piece = jax.ShapeDtypeStruct((SIDE, 2, 8, 768), jnp.float32)
    o0, o1, o2, o3 = pl.pallas_call(
        band_kernel,
        out_shape=[piece] * 4,
        in_specs=[smem()] * 3 + [vmem()] * 10,
        out_specs=[vmem()] * 4,
        scratch_shapes=[
            pltpu.VMEM((96, B, B), jnp.bfloat16),
            pltpu.VMEM((3, 256, 256), jnp.float32),
        ],
        compiler_params=params(24),
        name="bands",
    )(cols, aggs, agglo, split, split_rest, home, rest, near, near_2, lines_1, lines_3, pair, pair_rest)

    p2 = lax.ppermute(o2, BOTH, shift(2))
    p1 = lax.ppermute(o1, BOTH, shift(1))
    p3 = lax.ppermute(o3, BOTH, shift(3))
    kept, to_1, to_2, to_3 = (o0[m] + p1[m] + p3[m] + p2[m] for m in range(SIDE))
    q1 = lax.ppermute(to_1, BOTH, shift(1, 1))
    q3 = lax.ppermute(to_3, BOTH, shift(3, 1))
    q2 = lax.ppermute(to_2, BOTH, shift(2, 1))
    return (kept + q1 + q3 + q2).reshape(2, 8, 6, B)


def solution(mesh):
    placed = (
        P("row", "col", None, None),
        P("row", "col"),
        P(("row", "col"), None, None, None),
        P(),
        P(),
    )
    return jax.shard_map(
        local, mesh=mesh, in_specs=placed, out_specs=P("row", "col", None, None), check_vma=False
    )
```

```python
import functools

import jax
import jax.numpy as jnp
from jax import lax
from jax.experimental import pallas as pl
from jax.experimental.pallas import tpu as pltpu
from jax.sharding import PartitionSpec as P

ROWS = 16
SIDE = 4
B = 128
BOTH = ("row", "col")


def crossed(row):
    return (row + 1) // 2 % 2


def moved(along, move):
    pairs = []
    for r in range(ROWS):
        on_y = crossed(r) ^ along
        for y in range(SIDE):
            for x in range(SIDE):
                to = (move(y), x) if on_y else (y, move(x))
                pairs.append((r * ROWS + y * SIDE + x, r * ROWS + to[0] * SIDE + to[1]))
    return pairs


def shift(step, along=0):
    return moved(along, lambda c: (c + step) % SIDE)


def swap(k):
    return moved(1, lambda c: c ^ k)


def row_pairs(start):
    pairs = []
    for r in range(start, ROWS - 1, 2):
        pairs += [(r, r + 1), (r + 1, r)]
    return pairs


def place():
    row = lax.axis_index("row")
    col = lax.axis_index("col")
    return row, crossed(row), col // SIDE, col % SIDE


def slot_of(y, x, j, cross):
    y2, x2 = (j % ROWS) // SIDE, j % SIDE
    back = jnp.where(cross == 0, y ^ y2, x ^ x2)
    along = jnp.where(cross == 0, x - x2, y - y2) & 3
    return ((back >> 1) | ((back & 1) << 1)) * SIDE + along


def fetch_kernel(shard, near):
    near[...] = shard[...]


def row_at(y, x, slot, cross):
    back, along = (0, 2, 1, 3)[slot // SIDE], slot % SIDE
    y2 = jnp.where(cross == 0, y ^ back, (y - along) & 3)
    x2 = jnp.where(cross == 0, (x - along) & 3, x ^ back)
    return y2 * SIDE + x2


def lift_kernel(first_slot, aggs, agglo, a, blocks, split):
    row, cross, y, x = place()
    for p in range(ROWS // 2):
        i = row_at(y, x, first_slot + p, cross)
        swap = agglo[aggs[0, row * ROWS + i]] & 1
        left = jnp.concatenate([blocks[p * 2 + swap], blocks[p * 2 + 1 - swap]], axis=1)
        right = jnp.concatenate([a[i, 0], a[i, 1]], axis=1)
        lifted = lax.dot_general(
            left, right, (((0,), (0,)), ((), ())), preferred_element_type=jnp.float32
        )
        high = lifted.astype(jnp.bfloat16)
        low = (lifted - high.astype(jnp.float32)).astype(jnp.bfloat16)
        for s in range(2):
            split[p * 2 + s, :, :B] = high[:, s * B : (s + 1) * B]
            split[p * 2 + s, :, B:] = low[:, s * B : (s + 1) * B]


def band_kernel(
    cols, aggs, agglo, split, split_rest, home, rest, near, near_2, f, b, pair, pair_rest,
    o0, o1, o2, o3, blocks, acc
):
    row, cross, y, x = place()
    blocks[0:16] = home[...]
    blocks[16:32] = rest[...]
    blocks[32:40] = near[...]
    blocks[40:48] = near_2[...]
    blocks[48:56] = f[8:16]
    blocks[56:64] = b[8:16]
    blocks[64:80] = pair[...]
    blocks[80:96] = pair_rest[...]
    acc[...] = jnp.zeros_like(acc)
    pair_band = 2 - 2 * (row % 2)
    for p in range(ROWS):
        i = row_at(y, x, p, cross)
        part = split if p < ROWS // 2 else split_rest
        for s in range(2):
            j = cols[s, i]
            swap = agglo[aggs[0, j]] & 1
            band = j // ROWS - row + 1
            base = jnp.where(band == 1, 0, jnp.where(band == pair_band, 64, 32))
            spot = base + slot_of(y, x, j, jnp.where(band == pair_band, 1 - cross, cross)) * 2
            right = jnp.concatenate([blocks[spot + swap], blocks[spot + 1 - swap]], axis=1)
            right = jnp.concatenate([right, right], axis=0)
            acc[band] += jnp.dot(part[p % 8 * 2 + s], right, preferred_element_type=jnp.float32)
    for rel, out in enumerate((o0, o1, o2, o3)):
        for m in range(SIDE):
            d = jnp.where(
                cross == 0,
                ((y + m) & 3) * SIDE + ((x + rel) & 3),
                ((y + rel) & 3) * SIDE + ((x + m) & 3),
            )
            for k in range(2):
                start = pl.multiple_of(k * B + d * 8, 8)
                for t in range(3):
                    out[m, k, :, t * 256 : (t + 1) * 256] = acc[t, pl.ds(start, 8), :]


def vmem():
    return pl.BlockSpec(memory_space=pltpu.VMEM)


def smem():
    return pl.BlockSpec(memory_space=pltpu.SMEM)


def params(mib):
    return pltpu.CompilerParams(vmem_limit_bytes=mib * 2**20)


def local(a_blocks, a_cols, p_blocks, p_aggs, agglo):
    shard = p_blocks[0]
    across = lax.ppermute(shard, BOTH, swap(2))
    beside = lax.ppermute(shard, "row", row_pairs(1))
    shard_near = pl.pallas_call(
        fetch_kernel,
        out_shape=jax.ShapeDtypeStruct(shard.shape, shard.dtype),
        in_specs=[vmem()],
        out_specs=vmem(),
        compiler_params=params(8),
        name="fetch",
    )(shard)
    trio = jnp.concatenate([shard_near, beside, across])
    trio_1, trio_3, trio_2 = (lax.ppermute(trio, BOTH, shift(k)) for k in (1, 3, 2))
    line, near, line_2 = (
        jnp.concatenate([t[2 * n : 2 * n + 2] for t in (trio, trio_1, trio_2, trio_3)])
        for n in range(3)
    )
    lines = jnp.concatenate([line, near])
    lines_1 = lax.ppermute(lines, BOTH, swap(1))
    lines_3 = lax.ppermute(lines, BOTH, swap(3))
    near_2 = lax.ppermute(line_2, "row", row_pairs(1))
    home = jnp.concatenate([line, line_2])
    pair = lax.ppermute(home, "row", row_pairs(0))
    cols, aggs = a_cols.T, p_aggs.T

    def lift(first_slot, blocks, name):
        return pl.pallas_call(
            functools.partial(lift_kernel, first_slot),
            out_shape=jax.ShapeDtypeStruct((ROWS, 256, 256), jnp.bfloat16),
            in_specs=[smem(), smem(), vmem(), vmem()],
            out_specs=vmem(),
            compiler_params=params(16),
            name=name,
        )(aggs, agglo, a_blocks, blocks)

    split = lift(0, home, "lift_home")
    lines_1, lines_3, near_2, pair, split = lax.optimization_barrier(
        (lines_1, lines_3, near_2, pair, split)
    )
    rest = jnp.concatenate([lines_1[:8], lines_3[:8]])
    pair_rest = lax.ppermute(rest, "row", row_pairs(0))
    split_rest = lift(ROWS // 2, rest, "lift_rest")
    piece = jax.ShapeDtypeStruct((SIDE, 2, 8, 768), jnp.float32)
    o0, o1, o2, o3 = pl.pallas_call(
        band_kernel,
        out_shape=[piece] * 4,
        in_specs=[smem()] * 3 + [vmem()] * 10,
        out_specs=[vmem()] * 4,
        scratch_shapes=[
            pltpu.VMEM((96, B, B), jnp.bfloat16),
            pltpu.VMEM((3, 256, 256), jnp.float32),
        ],
        compiler_params=params(24),
        name="bands",
    )(cols, aggs, agglo, split, split_rest, home, rest, near, near_2, lines_1, lines_3, pair, pair_rest)

    p2 = lax.ppermute(o2, BOTH, shift(2))
    p1 = lax.ppermute(o1, BOTH, shift(1))
    p3 = lax.ppermute(o3, BOTH, shift(3))
    kept, to_1, to_2, to_3 = (o0[m] + p1[m] + p3[m] + p2[m] for m in range(SIDE))
    q2 = lax.ppermute(to_2, BOTH, shift(2, 1))
    q1 = lax.ppermute(to_1, BOTH, shift(1, 1))
    q3 = lax.ppermute(to_3, BOTH, shift(3, 1))
    return (kept + q1 + q3 + q2).reshape(2, 8, 6, B)


def solution(mesh):
    placed = (
        P("row", "col", None, None),
        P("row", "col"),
        P(("row", "col"), None, None, None),
        P(),
        P(),
    )
    return jax.shard_map(
        local, mesh=mesh, in_specs=placed, out_specs=P("row", "col", None, None), check_vma=False
    )
```

```python
import functools

import jax
import jax.numpy as jnp
from jax import lax
from jax.experimental import pallas as pl
from jax.experimental.pallas import tpu as pltpu
from jax.sharding import PartitionSpec as P

ROWS = 16
SIDE = 4
B = 128
BOTH = ("row", "col")


def crossed(row):
    return (row + 1) // 2 % 2


def moved(along, move):
    pairs = []
    for r in range(ROWS):
        on_y = crossed(r) ^ along
        for y in range(SIDE):
            for x in range(SIDE):
                to = (move(y), x) if on_y else (y, move(x))
                pairs.append((r * ROWS + y * SIDE + x, r * ROWS + to[0] * SIDE + to[1]))
    return pairs


def shift(step, along=0):
    return moved(along, lambda c: (c + step) % SIDE)


def swap(k):
    return moved(1, lambda c: c ^ k)


def row_pairs(start):
    pairs = []
    for r in range(start, ROWS - 1, 2):
        pairs += [(r, r + 1), (r + 1, r)]
    return pairs


def place():
    row = lax.axis_index("row")
    col = lax.axis_index("col")
    return row, crossed(row), col // SIDE, col % SIDE


def slot_of(y, x, j, cross):
    y2, x2 = (j % ROWS) // SIDE, j % SIDE
    back = jnp.where(cross == 0, y ^ y2, x ^ x2)
    along = jnp.where(cross == 0, x - x2, y - y2) & 3
    return ((back >> 1) | ((back & 1) << 1)) * SIDE + along


def fetch_kernel(shard, near):
    near[...] = shard[...]


def row_at(y, x, slot, cross):
    back, along = (0, 2, 1, 3)[slot // SIDE], slot % SIDE
    y2 = jnp.where(cross == 0, y ^ back, (y - along) & 3)
    x2 = jnp.where(cross == 0, (x - along) & 3, x ^ back)
    return y2 * SIDE + x2


def lift_kernel(first_slot, aggs, agglo, a, blocks, split):
    row, cross, y, x = place()
    for p in range(ROWS // 2):
        i = row_at(y, x, first_slot + p, cross)
        swap = agglo[aggs[0, row * ROWS + i]] & 1
        left = jnp.concatenate([blocks[p * 2 + swap], blocks[p * 2 + 1 - swap]], axis=1)
        right = jnp.concatenate([a[i, 0], a[i, 1]], axis=1)
        lifted = lax.dot_general(
            left, right, (((0,), (0,)), ((), ())), preferred_element_type=jnp.float32
        )
        high = lifted.astype(jnp.bfloat16)
        low = (lifted - high.astype(jnp.float32)).astype(jnp.bfloat16)
        for s in range(2):
            split[p * 2 + s, :, :B] = high[:, s * B : (s + 1) * B]
            split[p * 2 + s, :, B:] = low[:, s * B : (s + 1) * B]


def band_kernel(
    cols, aggs, agglo, split, split_rest, home, rest, near, near_2, f, b, pair, pair_1, pair_3,
    o0, o1, o2, o3, blocks, acc
):
    row, cross, y, x = place()
    blocks[0:16] = home[...]
    blocks[16:32] = rest[...]
    blocks[32:40] = near[...]
    blocks[40:48] = near_2[...]
    blocks[48:56] = f[8:16]
    blocks[56:64] = b[8:16]
    blocks[64:80] = pair[...]
    blocks[80:88] = pair_1[...]
    blocks[88:96] = pair_3[...]
    acc[...] = jnp.zeros_like(acc)
    pair_band = 2 - 2 * (row % 2)
    for p in range(ROWS):
        i = row_at(y, x, p, cross)
        part = split if p < ROWS // 2 else split_rest
        for s in range(2):
            j = cols[s, i]
            swap = agglo[aggs[0, j]] & 1
            band = j // ROWS - row + 1
            base = jnp.where(band == 1, 0, jnp.where(band == pair_band, 64, 32))
            spot = base + slot_of(y, x, j, jnp.where(band == pair_band, 1 - cross, cross)) * 2
            right = jnp.concatenate([blocks[spot + swap], blocks[spot + 1 - swap]], axis=1)
            right = jnp.concatenate([right, right], axis=0)
            acc[band] += jnp.dot(part[p % 8 * 2 + s], right, preferred_element_type=jnp.float32)
    for rel, out in enumerate((o0, o1, o2, o3)):
        for m in range(SIDE):
            d = jnp.where(
                cross == 0,
                ((y + m) & 3) * SIDE + ((x + rel) & 3),
                ((y + rel) & 3) * SIDE + ((x + m) & 3),
            )
            for k in range(2):
                start = pl.multiple_of(k * B + d * 8, 8)
                for t in range(3):
                    out[m, k, :, t * 256 : (t + 1) * 256] = acc[t, pl.ds(start, 8), :]


def vmem():
    return pl.BlockSpec(memory_space=pltpu.VMEM)


def smem():
    return pl.BlockSpec(memory_space=pltpu.SMEM)


def params(mib):
    return pltpu.CompilerParams(vmem_limit_bytes=mib * 2**20)


def local(a_blocks, a_cols, p_blocks, p_aggs, agglo):
    shard = p_blocks[0]
    across = lax.ppermute(shard, BOTH, swap(2))
    beside = lax.ppermute(shard, "row", row_pairs(1))
    shard_near = pl.pallas_call(
        fetch_kernel,
        out_shape=jax.ShapeDtypeStruct(shard.shape, shard.dtype),
        in_specs=[vmem()],
        out_specs=vmem(),
        compiler_params=params(8),
        name="fetch",
    )(shard)
    trio = jnp.concatenate([shard_near, across, beside])
    trio_1, trio_3, trio_2 = (lax.ppermute(trio, BOTH, shift(k)) for k in (1, 3, 2))
    line, line_2, near = (
        jnp.concatenate([t[2 * n : 2 * n + 2] for t in (trio, trio_1, trio_2, trio_3)])
        for n in range(3)
    )
    lines = jnp.concatenate([line, near])
    lines_1 = lax.ppermute(lines, BOTH, swap(1))
    lines_3 = lax.ppermute(lines, BOTH, swap(3))
    near_2 = lax.ppermute(line_2, "row", row_pairs(1))
    home = jnp.concatenate([line, line_2])
    pair = lax.ppermute(home, "row", row_pairs(0))
    cols, aggs = a_cols.T, p_aggs.T

    def lift(first_slot, blocks, name):
        return pl.pallas_call(
            functools.partial(lift_kernel, first_slot),
            out_shape=jax.ShapeDtypeStruct((ROWS, 256, 256), jnp.bfloat16),
            in_specs=[smem(), smem(), vmem(), vmem()],
            out_specs=vmem(),
            compiler_params=params(16),
            name=name,
        )(aggs, agglo, a_blocks, blocks)

    split = lift(0, home, "lift_home")
    lines_3, near_2, pair, split = lax.optimization_barrier((lines_3, near_2, pair, split))
    pair_3 = lax.ppermute(lines_3[:8], "row", row_pairs(0))
    pair_1 = lax.ppermute(lines_1[:8], "row", row_pairs(0))
    rest = jnp.concatenate([lines_1[:8], lines_3[:8]])
    split_rest = lift(ROWS // 2, rest, "lift_rest")
    piece = jax.ShapeDtypeStruct((SIDE, 2, 8, 768), jnp.float32)
    o0, o1, o2, o3 = pl.pallas_call(
        band_kernel,
        out_shape=[piece] * 4,
        in_specs=[smem()] * 3 + [vmem()] * 11,
        out_specs=[vmem()] * 4,
        scratch_shapes=[
            pltpu.VMEM((96, B, B), jnp.bfloat16),
            pltpu.VMEM((3, 256, 256), jnp.float32),
        ],
        compiler_params=params(24),
        name="bands",
    )(cols, aggs, agglo, split, split_rest, home, rest, near, near_2, lines_1, lines_3, pair, pair_1, pair_3)

    p2 = lax.ppermute(o2, BOTH, shift(2))
    p1 = lax.ppermute(o1, BOTH, shift(1))
    p3 = lax.ppermute(o3, BOTH, shift(3))
    kept, to_1, to_2, to_3 = (o0[m] + p1[m] + p3[m] + p2[m] for m in range(SIDE))
    q1 = lax.ppermute(to_1, BOTH, shift(1, 1))
    q3 = lax.ppermute(to_3, BOTH, shift(3, 1))
    q2 = lax.ppermute(to_2, BOTH, shift(2, 1))
    return (kept + q1 + q3 + q2).reshape(2, 8, 6, B)


def solution(mesh):
    placed = (
        P("row", "col", None, None),
        P("row", "col"),
        P(("row", "col"), None, None, None),
        P(),
        P(),
    )
    return jax.shard_map(
        local, mesh=mesh, in_specs=placed, out_specs=P("row", "col", None, None), check_vma=False
    )
```

```python
import functools

import jax
import jax.numpy as jnp
from jax import lax
from jax.experimental import pallas as pl
from jax.experimental.pallas import tpu as pltpu
from jax.sharding import PartitionSpec as P

ROWS = 16
SIDE = 4
B = 128
BOTH = ("row", "col")


def crossed(row):
    return (row + 1) // 2 % 2


def moved(along, move):
    pairs = []
    for r in range(ROWS):
        on_y = crossed(r) ^ along
        for y in range(SIDE):
            for x in range(SIDE):
                to = (move(y), x) if on_y else (y, move(x))
                pairs.append((r * ROWS + y * SIDE + x, r * ROWS + to[0] * SIDE + to[1]))
    return pairs


def shift(step, along=0):
    return moved(along, lambda c: (c + step) % SIDE)


def swap(k):
    return moved(1, lambda c: c ^ k)


def row_pairs(start):
    pairs = []
    for r in range(start, ROWS - 1, 2):
        pairs += [(r, r + 1), (r + 1, r)]
    return pairs


def place():
    row = lax.axis_index("row")
    col = lax.axis_index("col")
    return row, crossed(row), col // SIDE, col % SIDE


def slot_of(y, x, j, cross):
    y2, x2 = (j % ROWS) // SIDE, j % SIDE
    back = jnp.where(cross == 0, y ^ y2, x ^ x2)
    along = jnp.where(cross == 0, x - x2, y - y2) & 3
    return ((back >> 1) | ((back & 1) << 1)) * SIDE + along


def fetch_kernel(shard, near):
    near[...] = shard[...]


def row_at(y, x, slot, cross):
    back, along = (0, 2, 1, 3)[slot // SIDE], slot % SIDE
    y2 = jnp.where(cross == 0, y ^ back, (y - along) & 3)
    x2 = jnp.where(cross == 0, (x - along) & 3, x ^ back)
    return y2 * SIDE + x2


def lift_kernel(first_slot, aggs, agglo, a, blocks, split):
    row, cross, y, x = place()
    for p in range(ROWS // 2):
        i = row_at(y, x, first_slot + p, cross)
        swap = agglo[aggs[0, row * ROWS + i]] & 1
        left = jnp.concatenate([blocks[p * 2 + swap], blocks[p * 2 + 1 - swap]], axis=1)
        right = jnp.concatenate([a[i, 0], a[i, 1]], axis=1)
        lifted = lax.dot_general(
            left, right, (((0,), (0,)), ((), ())), preferred_element_type=jnp.float32
        )
        high = lifted.astype(jnp.bfloat16)
        low = (lifted - high.astype(jnp.float32)).astype(jnp.bfloat16)
        for s in range(2):
            split[p * 2 + s, :, :B] = high[:, s * B : (s + 1) * B]
            split[p * 2 + s, :, B:] = low[:, s * B : (s + 1) * B]


def band_kernel(
    cols, aggs, agglo, split, split_rest, home, rest, near, near_2, f, b, pair, pair_1, pair_3,
    o0, o1, o2, o3, blocks, acc
):
    row, cross, y, x = place()
    blocks[0:16] = home[...]
    blocks[16:32] = rest[...]
    blocks[32:40] = near[...]
    blocks[40:48] = near_2[...]
    blocks[48:56] = f[8:16]
    blocks[56:64] = b[8:16]
    blocks[64:80] = pair[...]
    blocks[80:88] = pair_1[...]
    blocks[88:96] = pair_3[...]
    acc[...] = jnp.zeros_like(acc)
    pair_band = 2 - 2 * (row % 2)
    for p in range(ROWS):
        i = row_at(y, x, p, cross)
        part = split if p < ROWS // 2 else split_rest
        for s in range(2):
            j = cols[s, i]
            swap = agglo[aggs[0, j]] & 1
            band = j // ROWS - row + 1
            base = jnp.where(band == 1, 0, jnp.where(band == pair_band, 64, 32))
            spot = base + slot_of(y, x, j, jnp.where(band == pair_band, 1 - cross, cross)) * 2
            right = jnp.concatenate([blocks[spot + swap], blocks[spot + 1 - swap]], axis=1)
            right = jnp.concatenate([right, right], axis=0)
            acc[band] += jnp.dot(part[p % 8 * 2 + s], right, preferred_element_type=jnp.float32)
    for rel, out in enumerate((o0, o1, o2, o3)):
        for m in range(SIDE):
            d = jnp.where(
                cross == 0,
                ((y + m) & 3) * SIDE + ((x + rel) & 3),
                ((y + rel) & 3) * SIDE + ((x + m) & 3),
            )
            for k in range(2):
                start = pl.multiple_of(k * B + d * 8, 8)
                for t in range(3):
                    out[m, k, :, t * 256 : (t + 1) * 256] = acc[t, pl.ds(start, 8), :]


def vmem():
    return pl.BlockSpec(memory_space=pltpu.VMEM)


def smem():
    return pl.BlockSpec(memory_space=pltpu.SMEM)


def params(mib):
    return pltpu.CompilerParams(vmem_limit_bytes=mib * 2**20)


def local(a_blocks, a_cols, p_blocks, p_aggs, agglo):
    shard = p_blocks[0]
    across = lax.ppermute(shard, BOTH, swap(2))
    beside = lax.ppermute(shard, "row", row_pairs(1))
    shard_near = pl.pallas_call(
        fetch_kernel,
        out_shape=jax.ShapeDtypeStruct(shard.shape, shard.dtype),
        in_specs=[vmem()],
        out_specs=vmem(),
        compiler_params=params(8),
        name="fetch",
    )(shard)
    trio = jnp.concatenate([shard_near, across, beside])
    trio_1, trio_3, trio_2 = (lax.ppermute(trio, BOTH, shift(k)) for k in (1, 3, 2))
    line, line_2, near = (
        jnp.concatenate([t[2 * n : 2 * n + 2] for t in (trio, trio_1, trio_2, trio_3)])
        for n in range(3)
    )
    lines = jnp.concatenate([line, near])
    lines_1 = lax.ppermute(lines, BOTH, swap(1))
    lines_3 = lax.ppermute(lines, BOTH, swap(3))
    near_2 = lax.ppermute(line_2, "row", row_pairs(1))
    home = jnp.concatenate([line, line_2])
    pair = lax.ppermute(home, "row", row_pairs(0))
    cols, aggs = a_cols.T, p_aggs.T

    def lift(first_slot, blocks, name):
        return pl.pallas_call(
            functools.partial(lift_kernel, first_slot),
            out_shape=jax.ShapeDtypeStruct((ROWS, 256, 256), jnp.bfloat16),
            in_specs=[smem(), smem(), vmem(), vmem()],
            out_specs=vmem(),
            compiler_params=params(16),
            name=name,
        )(aggs, agglo, a_blocks, blocks)

    split = lift(0, home, "lift_home")
    lines_1, near_2, pair, split = lax.optimization_barrier((lines_1, near_2, pair, split))
    pair_3 = lax.ppermute(lines_3[:8], "row", row_pairs(0))
    pair_1 = lax.ppermute(lines_1[:8], "row", row_pairs(0))
    rest = jnp.concatenate([lines_1[:8], lines_3[:8]])
    split_rest = lift(ROWS // 2, rest, "lift_rest")
    piece = jax.ShapeDtypeStruct((SIDE, 2, 8, 768), jnp.float32)
    o0, o1, o2, o3 = pl.pallas_call(
        band_kernel,
        out_shape=[piece] * 4,
        in_specs=[smem()] * 3 + [vmem()] * 11,
        out_specs=[vmem()] * 4,
        scratch_shapes=[
            pltpu.VMEM((96, B, B), jnp.bfloat16),
            pltpu.VMEM((3, 256, 256), jnp.float32),
        ],
        compiler_params=params(24),
        name="bands",
    )(cols, aggs, agglo, split, split_rest, home, rest, near, near_2, lines_1, lines_3, pair, pair_1, pair_3)

    p2 = lax.ppermute(o2, BOTH, shift(2))
    p1 = lax.ppermute(o1, BOTH, shift(1))
    p3 = lax.ppermute(o3, BOTH, shift(3))
    kept, to_1, to_2, to_3 = (o0[m] + p1[m] + p3[m] + p2[m] for m in range(SIDE))
    q1 = lax.ppermute(to_1, BOTH, shift(1, 1))
    q3 = lax.ppermute(to_3, BOTH, shift(3, 1))
    q2 = lax.ppermute(to_2, BOTH, shift(2, 1))
    return (kept + q1 + q3 + q2).reshape(2, 8, 6, B)


def solution(mesh):
    placed = (
        P("row", "col", None, None),
        P("row", "col"),
        P(("row", "col"), None, None, None),
        P(),
        P(),
    )
    return jax.shard_map(
        local, mesh=mesh, in_specs=placed, out_specs=P("row", "col", None, None), check_vma=False
    )
```
